512 devices in a mesh: mp: 2 (over core), tp: 8 (over z_lo), lat: 32 (over x, y, z_hi).
Axes of the slice: x: 4, y: 4, z: 16 (z_hi: 2, z_lo: 8; z = z_hi * 8 + z_lo), core: 2. Of those that a mesh axis runs over, the one named last changes fastest.
Arguments:
- resid_in: bfloat16 [2, 384, 3584], P('mp', 'lat'), may hold values from -6 to 6
- pre_gain: bfloat16 [2, 3584], P('mp'), may hold values from 0.25 to 1.75
- w_gate: bfloat16 [2, 14336, 3584], P('mp', 'lat', 'tp'), may hold values from -0.09375 to 0.09375
- w_up: bfloat16 [2, 14336, 3584], P('mp', 'lat', 'tp'), may hold values from -0.09375 to 0.09375
- w_down: bfloat16 [2, 14336, 3584], P('mp', 'lat', 'tp'), may hold values from -1 to 1
- post_gain: bfloat16 [2, 3584], P('mp', 'tp'), may hold values from 0.25 to 1.75
- enc_weight: bfloat16 [2, 3584, 32768], P('mp', 'tp', 'lat'), may hold values from -0.0625 to 0.0625
- enc_bias: bfloat16 [32768], P('lat'), may hold values from -3 to 3
- dec_weight: bfloat16 [2, 3584, 32768], P('mp', 'tp', 'lat'), may hold values from -0.03125 to 0.03125
- dec_bias: bfloat16 [2, 3584], P('mp', 'tp'), may hold values from -3 to 3
- prompt_of_row: int32 [384], replicated, may hold values from 0 to 95, never falling along the last dimension, each value on 1 to 8 neighbouring positions
- pad_mask: int32 [384], replicated, may hold values 0 or 1
- pair_ids: int32 [96], replicated, may hold values from 0 to 95, each once
Outputs:
- enc_grad: bfloat16 [2, 3584, 32768], P('mp', 'tp', 'lat')
- dec_grad: bfloat16 [2, 3584, 32768], P('mp', 'tp', 'lat')
The draws below stay inside these ranges and needn't reach their ends.
Inputs may be any that keep to these rules, and one draw needn't show every extreme that they name: `prompt_of_row`: never falls from one row to the next; each of the 96 prompts has 1 to 8 rows, one exactly 8. `pair_ids`: each slot once; the prompts in slots 2k and 2k + 1 form pair k.
All inputs are finite; a program needn't handle non-finite values.
Results may differ from the reference program's by a relative error of at most 0.014.
Values may be sent and summed in bfloat16 or wider, within the bound.
A program may use at most 64 MiB of HBM per device.

```python
import math
import jax
import jax.numpy as jnp
import numpy as np
from jax import lax

D = 3584
FF = 14336
LATENTS = 32768
TOKENS = 384
PROMPTS = 96
SEG_MOST = 8
N_LAT = 32


def scaled_columns(key, entries, low_scale, high_scale):
    columns = jnp.arange(D, dtype=jnp.float32) / (D - 1)
    col_scale = jnp.exp(jnp.log(low_scale) + columns * (jnp.log(high_scale) - jnp.log(low_scale)))
    ff_block = jnp.arange(FF, dtype=jnp.int32) // (FF // N_LAT)
    d_block = jnp.arange(D, dtype=jnp.int32) // (D // N_LAT)
    paired = jax.random.permutation(jax.random.fold_in(key, 11), N_LAT).astype(jnp.int32)
    spike = jnp.where(paired[ff_block][:, None] == d_block[None, :], 3.0, 1.0)
    return entries * col_scale[None, None, :] * spike[None, :, :] * FF ** (-0.5)


def draw_w_down(key, part):
    key = jax.random.fold_in(key, 7)
    entries = jnp.clip(jax.random.normal(key, (2, FF, D), jnp.float32), -6.0, 6.0)
    values = scaled_columns(key, entries, 0.5, 2.0)
    return jnp.clip(values, -1.0, 1.0).astype(jnp.bfloat16)


def with_ends(values, rng, low, top_value):
    longest = values.shape.index(max(values.shape))
    spots = []
    for shift in (0, 1):
        where = [jax.random.randint(jax.random.fold_in(rng, axis), (), 0, length) for axis, length in enumerate(values.shape)]
        where[longest] = (where[longest] + shift) % values.shape[longest]
        spots.append(tuple(where))
    return values.at[spots[0]].set(low).at[spots[1]].set(top_value)


def level_of(key, shape, shards, least, largest):
    def one(axis_at, shards_of):
        steps = jax.random.uniform(jax.random.fold_in(jax.random.fold_in(key, 6), axis_at), (shards_of,), jnp.float32, least / len(shards), largest / len(shards))
        return jnp.repeat(jnp.exp(steps), shape[axis_at] // shards_of).reshape((-1,) + (1,) * (len(shape) - axis_at - 1))

    loudness = one(*shards[0])
    for cut in shards[1:]:
        loudness = loudness * one(*cut)
    return loudness


def length_profile(number_of, total, limit, lean):
    weights = [(1 << 20) // math.isqrt(grade ** lean) + 1 for grade in range(2, number_of + 1)]
    surplus, holding = total - limit - (number_of - 1), [1] * (number_of - 1)
    while surplus > 0:
        movable = [i for i in range(number_of - 1) if holding[i] < limit]
        pool, remaining = sum([weights[i] for i in movable]), surplus
        for i in movable:
            extra = min(limit - holding[i], max(1, remaining * weights[i] // pool), surplus)
            holding[i] = holding[i] + extra
            surplus = surplus - extra
    return np.array([limit] + holding)


def uneven_parts(rng, number_of, total, bound, lean):
    if number_of == 2:
        one = jax.random.randint(rng, (), max(1, total - bound), min(bound, total - 1) + 1)
        return jnp.stack([one, total - one])
    lengths = jnp.asarray(length_profile(number_of, total, bound, lean), jnp.int32)
    twos = (number_of - 1) // 2
    source_of, receiver = lengths[1:1 + 2 * twos:2], lengths[2:2 + 2 * twos:2]
    margin = jnp.minimum(source_of - 1, bound - receiver)
    moved = jax.random.randint(jax.random.fold_in(rng, 1), (twos,), 0, 1 << 20) % (margin + 1)
    lengths = lengths.at[1:1 + 2 * twos:2].set(source_of - moved).at[2:2 + 2 * twos:2].set(receiver + moved)
    return lengths[jax.random.permutation(jax.random.fold_in(rng, 2), number_of)]


def centred(own_key, dims, scale, bound, pieces=(), held_as=jnp.bfloat16):
    values = jax.random.normal(own_key, dims, jnp.float32) * scale
    if len(pieces) > 0:
        values = level_of(own_key, dims, pieces, -0.22, 0.18) * values
    return jnp.clip(values, min=-bound, max=bound).astype(held_as)


def setup_inputs(seed: int = 0) -> dict:
    key_of = jax.random.split(jax.random.key(seed), 14)
    resid_in = centred(key_of[0], (2, TOKENS, D), 1.0, 6.0, ((0, 2), (1, 32)))
    pre_gain = jnp.clip(1.0 + 0.15 * jax.random.normal(key_of[1], (2, D), jnp.float32), 0.25, 1.75).astype(jnp.bfloat16)
    w_gate = centred(key_of[2], (2, FF, D), D ** -0.5, 0.09375, ((0, 2), (1, 32), (2, 8)))
    w_up = centred(key_of[3], (2, FF, D), D ** -0.5, 0.09375, ((0, 2), (1, 32), (2, 8)))
    w_down = draw_w_down(jax.random.fold_in(key_of[13], 71), 0)
    post_gain = jnp.clip(1.0 + 0.15 * jax.random.normal(key_of[5], (2, D), jnp.float32), 0.25, 1.75).astype(jnp.bfloat16)
    enc_weight = centred(key_of[6], (2, D, LATENTS), (2 * D) ** -0.5, 0.0625, ((0, 2), (1, 8), (2, 32)))
    enc_bias = centred(key_of[7], (LATENTS,), 0.5, 3.0, ((0, 32),))
    dec_weight = centred(key_of[8], (2, D, LATENTS), LATENTS ** -0.5, 0.03125, ((0, 2), (1, 8), (2, 32)))
    dec_bias = centred(key_of[9], (2, D), 0.5, 3.0, ((0, 2), (1, 8)))
    prompt_of_row = jnp.searchsorted(jnp.cumsum(uneven_parts(key_of[10], PROMPTS, TOKENS, SEG_MOST, 0)), jnp.arange(TOKENS), side="right").astype(jnp.int32)
    pad_mask = with_ends((jax.random.randint(key_of[11], (TOKENS,), 0, 8) < 7).astype(jnp.int32), jax.random.fold_in(key_of[11], 1), 0, 1)
    pair_ids = jax.random.permutation(key_of[12], PROMPTS).astype(jnp.int32)
    return {"resid_in": resid_in, "pre_gain": pre_gain, "w_gate": w_gate, "w_up": w_up, "w_down": w_down, "post_gain": post_gain, "enc_weight": enc_weight, "enc_bias": enc_bias, "dec_weight": dec_weight, "dec_bias": dec_bias, "prompt_of_row": prompt_of_row, "pad_mask": pad_mask, "pair_ids": pair_ids}


norm_eps = 1e-06

def rms_scale(values):
    return lax.rsqrt(lax.optimization_barrier(jnp.mean(values * values, axis=-1, keepdims=True)) + norm_eps)

def row_weights(prompt_of_row, pad_mask, pair_ids):
    prompt_count = pair_ids.shape[0]
    pair_count = prompt_count // 2
    pair_of_prompt = (pair_ids // 2).astype(jnp.int32)
    in_prompt = prompt_of_row[:, None] == jnp.arange(prompt_count, dtype=jnp.int32)[None, :]
    pair_of_row = lax.optimization_barrier(jnp.sum(jnp.where(in_prompt, pair_of_prompt[None, :], 0), axis=1)).astype(jnp.int32)
    in_pair = pair_of_row[:, None] == jnp.arange(pair_count, dtype=jnp.int32)[None, :]
    valid = pad_mask.astype(jnp.float32)
    counts = lax.optimization_barrier(jnp.sum(jnp.where(in_pair, valid[:, None], jnp.float32(0.0)), axis=0))
    inverse = 1.0 / jnp.maximum(counts, jnp.float32(1.0))
    return valid * lax.optimization_barrier(jnp.sum(jnp.where(in_pair, inverse[None, :], jnp.float32(0.0)), axis=1))

def block_layer(inputs, pre_gain, w_gate, w_up, w_down, post_gain):
    inputs_f = inputs.astype(jnp.float32)
    normed = (inputs_f * rms_scale(inputs_f) * pre_gain.astype(jnp.float32)).astype(jnp.bfloat16)
    gate_out = jnp.dot(normed, w_gate.T, preferred_element_type=jnp.float32)
    upward = jnp.dot(normed, w_up.T, preferred_element_type=jnp.float32)
    hidden = (jax.nn.gelu(gate_out, approximate=True) * upward).astype(jnp.bfloat16)
    mixed = jnp.dot(hidden, w_down, preferred_element_type=jnp.float32)
    return (inputs_f + mixed * rms_scale(mixed) * post_gain.astype(jnp.float32)).astype(jnp.bfloat16)

def reference(resid_in, pre_gain, w_gate, w_up, w_down, post_gain, enc_weight, enc_bias, dec_weight, dec_bias, prompt_of_row, pad_mask, pair_ids):
    resid = [block_layer(resid_in[model], pre_gain[model], w_gate[model], w_up[model], w_down[model], post_gain[model]) for model in range(2)]
    pre_act = enc_bias.astype(jnp.float32)[None, :]
    for model in range(2):
        pre_act = pre_act + jnp.dot(resid[model], enc_weight[model], preferred_element_type=jnp.float32)
    active = jnp.maximum(pre_act, jnp.float32(0.0))
    features = (active * active).astype(jnp.bfloat16)
    col_norms = jnp.sqrt(lax.optimization_barrier(jnp.sum(jnp.square(dec_weight.astype(jnp.float32)), axis=1)) + norm_eps)
    norm_total = col_norms[0] + col_norms[1]
    weight_rows = row_weights(prompt_of_row, pad_mask, pair_ids)
    weighted = lax.optimization_barrier(jnp.sum(weight_rows[:, None] * features.astype(jnp.float32), axis=0))
    back_prop = weight_rows[:, None] * norm_total[None, :]
    dec_grads = []
    for model in range(2):
        recon = jnp.dot(features, dec_weight[model].T, preferred_element_type=jnp.float32) + dec_bias[model].astype(jnp.float32)[None, :]
        recon_error = recon - resid[model].astype(jnp.float32)
        err_grad = (2.0 * weight_rows[:, None] * recon_error).astype(jnp.bfloat16)
        direct = jnp.dot(err_grad.T, features, preferred_element_type=jnp.float32)
        dec_grads.append((direct + weighted[None, :] * dec_weight[model].astype(jnp.float32) / col_norms[model][None, :]).astype(jnp.bfloat16))
        back_prop = back_prop + jnp.dot(err_grad, dec_weight[model], preferred_element_type=jnp.float32)
    pre_grad = (back_prop * 2.0 * active).astype(jnp.bfloat16)
    enc_grads = [jnp.dot(resid[model].T, pre_grad, preferred_element_type=jnp.float32).astype(jnp.bfloat16) for model in range(2)]
    return (jnp.stack(enc_grads), jnp.stack(dec_grads))
```

```python
import functools

import jax
import jax.numpy as jnp
from jax import lax
from jax.experimental import pallas as pl
from jax.experimental.pallas import tpu as pltpu
from jax.sharding import PartitionSpec as P

MESH = pl.DeviceIdType.MESH
f32, bf16 = jnp.float32, jnp.bfloat16
EPS = 1e-06
NB = 3
ROWS = 384
R = ROWS // NB
RZ = R // 8
RX = R // 16
CW = 448
LW = 1024
HL = 512

LAST = (((1,), (1,)), ((), ()))
PLAIN = (((1,), (0,)), ((), ()))
FIRST = (((0,), (0,)), ((), ()))


def dot(a, b, dims=PLAIN):
    return lax.dot_general(a, b, dims, preferred_element_type=f32)


def merge(v, rows):
    return v.astype(f32).reshape(rows, v.shape[-1]).astype(bf16)


SCRATCH = {
    "payload": pltpu.VMEM((2, 12, 512), bf16),
    "own24": pltpu.VMEM((24, 512), f32),
    "nx": pltpu.VMEM((16, 24, 512), bf16),
    "xf": pltpu.VMEM((ROWS, 512), f32),
    "wgu": pltpu.VMEM((2 * CW, CW), bf16),
    "wrow": pltpu.VMEM((ROWS, 128), f32),
    "nsq": pltpu.VMEM((8, 1, LW), f32),
    "cn": pltpu.VMEM((2, 1, LW), f32),
    "pg": pltpu.VMEM((NB, 8, RZ, 2 * CW), bf16),
    "rg": pltpu.VMEM((NB, 8, RZ, 2 * CW), bf16),
    "hd": pltpu.VMEM((NB, 8, RZ, CW), bf16),
    "pm": pltpu.VMEM((2, NB, 16, RX, CW), bf16),
    "rm": pltpu.VMEM((2, NB, 16, RX, CW), bf16),
    "hs": pltpu.VMEM((2, NB, RX, CW), bf16),
    "hr": pltpu.VMEM((2, NB, RX, CW), bf16),
    "sq": pltpu.VMEM((NB, 8, RX, 128), f32),
    "rsd": pltpu.VMEM((NB, 16, RX, CW), bf16),
    "err": pltpu.VMEM((NB, 16, RX, CW), bf16),
    "ms": pltpu.VMEM((2, NB, R, HL), bf16),
    "mr": pltpu.VMEM((2, NB, R, HL), bf16),
    "pe": pltpu.VMEM((2, NB, 8, RZ, HL), bf16),
    "re": pltpu.VMEM((2, NB, 8, RZ, HL), bf16),
    "act": pltpu.VMEM((NB, RZ, HL), f32),
    "fe": pltpu.VMEM((NB, 2, 8, RZ, HL), bf16),
    "pd": pltpu.VMEM((NB, 2, 8, RZ, HL), bf16),
    "sem": pltpu.SemaphoreType.DMA((2, 200 * NB + 40)),
}


def kernel(*refs):
    (x_ref, pre_ref, wg_ref, wu_ref, wd_ref, post_ref, ew_ref, eb_ref, dw_ref, db_ref,
     prompt_ref, pad_ref, ids_ref, eg_ref, dg_ref) = refs[:15]
    s = dict(zip(SCRATCH, refs[15:]))
    sem = s["sem"]
    m, i, lat = lax.axis_index("mp"), lax.axis_index("tp"), lax.axis_index("lat")
    q, h = lax.div(lat, 2), lax.rem(lat, 2)
    to_z = [{"tp": lax.rem(i + k, 8)} for k in range(1, 8)]
    to_q = [lax.rem(q + k, 16) for k in range(1, 16)]
    to_xy = [{"lat": 2 * p + h} for p in to_q]
    to_h = {"lat": 2 * q + 1 - h}
    to_m = {"mp": 1 - m}

    gate = pltpu.get_barrier_semaphore()
    everyone = to_z + to_xy + [to_h, to_m]
    for d in everyone:
        pl.semaphore_signal(gate, inc=1, device_id=d, device_id_type=MESH)

    used, sends = [0], []

    def send(src, dst, where):
        n = used[0]
        used[0] += 1
        c = pltpu.make_async_remote_copy(
            src_ref=src, dst_ref=dst, send_sem=sem.at[0, n], recv_sem=sem.at[1, n],
            device_id=where, device_id_type=MESH)
        c.start()
        sends.append(c)
        return c

    def wait(copies):
        for c in copies:
            c.wait_recv()

    def z_scatter(src, dst):
        return [send(src.at[lax.rem(i + k, 8)], dst.at[k], to_z[k - 1]) for k in range(1, 8)]

    def z_gather(ref):
        return [send(ref.at[i], ref.at[i], to_z[k - 1]) for k in range(1, 8)]

    def xy_scatter(src, dst):
        return [send(src.at[to_q[k - 1]], dst.at[k], to_xy[k - 1]) for k in range(1, 16)]

    def xy_gather(ref):
        return [send(ref.at[q], ref.at[q], to_xy[k - 1]) for k in range(1, 16)]

    def total(own, ref, count):
        acc = own.astype(f32)
        for k in range(1, count):
            acc = acc + ref[k].astype(f32)
        return acc

    x = x_ref[0].astype(f32)
    scale = lax.rsqrt(jnp.sum(x * x, axis=1, keepdims=True) / (8 * CW) + EPS)
    p0 = scale.astype(bf16).astype(f32)
    p1 = (scale - p0).astype(bf16).astype(f32)
    p2 = scale - p0 - p1
    cols = jnp.zeros((12, CW), f32)
    gain_in = jnp.zeros((1, CW), f32)
    pre = pre_ref[...].astype(f32)
    for c in range(8):
        cols = jnp.where(i == c, x[:, c * CW:(c + 1) * CW], cols)
        gain_in = jnp.where(i == c, pre[:, c * CW:(c + 1) * CW], gain_in)
    payload = jnp.concatenate([cols, jnp.zeros((12, 64), f32)], axis=1)
    lane = lax.broadcasted_iota(jnp.int32, (12, 512), 1)
    payload = jnp.where(lane == CW, p0, jnp.where(lane == CW + 1, p1, jnp.where(lane == CW + 2, p2, payload)))
    s["payload"][h] = payload.astype(bf16)

    dw = dw_ref[0].astype(f32)
    s["nsq"][i] = jnp.sum(dw * dw, axis=0, keepdims=True)

    pl.semaphore_wait(gate, len(everyone))

    wait([send(s["payload"].at[h], s["payload"].at[h], to_h)])
    s["own24"][0:12] = s["payload"][0].astype(f32)
    s["own24"][12:24] = s["payload"][1].astype(f32)
    s["nx"][q] = s["own24"][...].astype(bf16)
    x_copies = xy_gather(s["nx"])
    norm_copies = z_gather(s["nsq"])

    def column(v):
        return jnp.broadcast_to(v, (128, v.shape[1])).T[:, :1]

    prompt = column(prompt_ref[...])
    valid = column(pad_ref[...].astype(f32))
    in_prompt = prompt == lax.broadcasted_iota(jnp.int32, (ROWS, 96), 1)
    pair_of_prompt = lax.shift_right_logical(ids_ref[...], 1).astype(f32)
    pair = jnp.sum(jnp.where(in_prompt, pair_of_prompt, 0.0), axis=1, keepdims=True)
    in_pair = pair == lax.broadcasted_iota(jnp.int32, (ROWS, 48), 1).astype(f32)
    counts = jnp.sum(jnp.where(in_pair, valid, 0.0), axis=0, keepdims=True)
    inverse = 1.0 / jnp.maximum(counts, 1.0)
    wrow = valid * jnp.sum(jnp.where(in_pair, inverse, 0.0), axis=1, keepdims=True)
    s["wrow"][...] = jnp.broadcast_to(wrow, (ROWS, 128))
    s["wgu"][0:CW] = wg_ref[0]
    s["wgu"][CW:2 * CW] = wu_ref[0]

    post = post_ref[...].astype(f32)
    dbias = db_ref[...].astype(f32)
    half = pl.ds(pl.multiple_of(m * HL, HL), HL)
    other = pl.ds(pl.multiple_of((1 - m) * HL, HL), HL)

    wait(x_copies)
    s["xf"][...] = s["nx"][...].astype(f32).reshape(ROWS, 512)

    def mp_and_tp_sum(b, t, left, weight):
        s["ms"][t, b] = dot(left, weight[0, :, other]).astype(bf16)
        c = send(s["ms"].at[t, b], s["mr"].at[t, b], to_m)
        mine = dot(left, weight[0, :, half])
        c.wait_recv()
        both = mine + s["mr"][t, b].astype(f32)
        s["pe"][t, b] = both.reshape(8, RZ, HL).astype(bf16)
        return z_scatter(s["pe"].at[t, b], s["re"].at[t, b])

    def lat_sum(b, t, part):
        s["pm"][t, b] = part.reshape(16, RX, CW).astype(bf16)
        return xy_scatter(s["pm"].at[t, b], s["rm"].at[t, b])

    def block(b):
        rows = slice(b * R, (b + 1) * R)
        own_x = pl.ds(pl.multiple_of(b * R + q * RX, 8), RX)
        own_z = pl.ds(pl.multiple_of(b * R + i * RZ, 8), RZ)
        xb = s["xf"][rows]
        row_scale = xb[:, CW:CW + 1] + xb[:, CW + 1:CW + 2] + xb[:, CW + 2:CW + 3]
        normed = (xb[:, :CW] * row_scale * gain_in).astype(bf16)
        s["pg"][b] = dot(normed, s["wgu"][...], LAST).reshape(8, RZ, 2 * CW).astype(bf16)
        c = z_scatter(s["pg"].at[b], s["rg"].at[b])
        yield
        wait(c)
        both = total(s["pg"][b, i], s["rg"].at[b], 8)
        g, u = both[:, :CW], both[:, CW:]
        s["hd"][b, i] = (0.5 * g * (1.0 + jnp.tanh(0.7978845608028654 * (g + 0.044715 * g * g * g))) * u).astype(bf16)
        c = z_gather(s["hd"].at[b])
        yield
        wait(c)
        c = lat_sum(b, 0, dot(merge(s["hd"][b], R), wd_ref[0]))
        yield
        wait(c)
        s["hs"][0, b] = total(s["pm"][0, b, q], s["rm"].at[0, b], 16).astype(bf16)
        c = [send(s["hs"].at[0, b], s["hr"].at[0, b], to_h)]
        yield
        wait(c)
        mixed = s["hs"][0, b].astype(f32) + s["hr"][0, b].astype(f32)
        s["sq"][b, i] = jnp.broadcast_to(jnp.sum(mixed * mixed, axis=1, keepdims=True), (RX, 128))
        c = z_gather(s["sq"].at[b])
        yield
        wait(c)
        square = s["sq"][b, 0]
        for k in range(1, 8):
            square = square + s["sq"][b, k]
        out_scale = lax.rsqrt(square[:, :1] / (8 * CW) + EPS)
        s["rsd"][b, q] = (s["xf"][own_x, :][:, :CW] + mixed * out_scale * post).astype(bf16)
        c = xy_gather(s["rsd"].at[b])
        yield
        wait(c)
        c = mp_and_tp_sum(b, 0, merge(s["rsd"][b], R), ew_ref)
        yield
        wait(c)
        pre_act = total(s["pe"][0, b, i], s["re"].at[0, b], 8) + eb_ref[:, half].astype(f32)
        active = jnp.maximum(pre_act, 0.0)
        s["act"][b] = active
        s["fe"][b, m, i] = (active * active).astype(bf16)
        c = z_gather(s["fe"].at[b, m])
        yield
        wait(c)
        c = [send(s["fe"].at[b, m], s["fe"].at[b, m], to_m)]
        yield
        wait(c)
        recon = dot(merge(s["fe"][b, 0], R), dw_ref[0, :, :HL], LAST)
        recon = recon + dot(merge(s["fe"][b, 1], R), dw_ref[0, :, HL:], LAST)
        c = lat_sum(b, 1, recon)
        yield
        wait(c)
        s["hs"][1, b] = total(s["pm"][1, b, q], s["rm"].at[1, b], 16).astype(bf16)
        c = [send(s["hs"].at[1, b], s["hr"].at[1, b], to_h)]
        yield
        wait(c)
        error = s["hs"][1, b].astype(f32) + s["hr"][1, b].astype(f32) + dbias - s["rsd"][b, q].astype(f32)
        s["err"][b, q] = (2.0 * s["wrow"][own_x, :][:, :1] * error).astype(bf16)
        c = xy_gather(s["err"].at[b])
        yield
        wait(c)
        c = mp_and_tp_sum(b, 1, merge(s["err"][b], R), dw_ref)
        yield
        wait(c)
        norm_total = s["cn"][0, :, half] + s["cn"][1, :, half]
        grad = total(s["pe"][1, b, i], s["re"].at[1, b], 8) + s["wrow"][own_z, :][:, :1] * norm_total
        s["pd"][b, m, i] = (grad * 2.0 * s["act"][b]).astype(bf16)
        c = z_gather(s["pd"].at[b, m])
        yield
        wait(c)
        c = [send(s["pd"].at[b, m], s["pd"].at[b, m], to_m)]
        yield
        wait(c)

    running = [block(b) for b in range(NB)]
    phase = 0
    while running:
        running = [g for g in running if next(g, True) is None]
        phase += 1
        if phase == 2:
            wait(norm_copies)
            squares = s["nsq"][0]
            for k in range(1, 8):
                squares = squares + s["nsq"][k]
            s["cn"][m] = jnp.sqrt(squares + EPS)
            cn_copy = send(s["cn"].at[m], s["cn"].at[m], to_m)
        if phase == 3:
            cn_copy.wait_recv()
        if phase == 14:
            err = merge(s["err"][...], ROWS)
            own_norm = s["cn"][m]
            for p in range(2):
                at = slice(p * HL, (p + 1) * HL)
                feats = s["fe"][:, p].astype(f32).reshape(ROWS, HL)
                weighted = jnp.sum(s["wrow"][:, :1] * feats, axis=0, keepdims=True)
                direct = dot(err, feats.astype(bf16), FIRST)
                dg_ref[0, :, at] = (
                    direct + weighted * dw_ref[0, :, at].astype(f32) / own_norm[:, at]).astype(bf16)

    resid = merge(s["rsd"][...], ROWS)
    for p in range(2):
        at = slice(p * HL, (p + 1) * HL)
        eg_ref[0, :, at] = dot(resid, merge(s["pd"][:, p], ROWS), FIRST).astype(bf16)
    for c in sends:
        c.wait_send()


def local(*args):
    args = list(args)
    for n in (7, 10, 11, 12):
        args[n] = args[n][None]
    vmem = pl.BlockSpec(memory_space=pltpu.VMEM)
    out = jax.ShapeDtypeStruct((1, CW, LW), bf16)
    return pl.pallas_call(
        kernel,
        out_shape=(out, out),
        in_specs=[vmem] * 13,
        out_specs=(vmem, vmem),
        scratch_shapes=list(SCRATCH.values()),
        compiler_params=pltpu.CompilerParams(
            collective_id=1, has_side_effects=True, vmem_limit_bytes=56 << 20),
        cost_estimate=pl.CostEstimate(flops=2300000000, bytes_accessed=7000000, transcendentals=100000),
    )(*args)


def solution(mesh):
    placed = (
        P("mp", "lat", None),
        P("mp", None),
        P("mp", "lat", "tp"),
        P("mp", "lat", "tp"),
        P("mp", "lat", "tp"),
        P("mp", "tp"),
        P("mp", "tp", "lat"),
        P("lat"),
        P("mp", "tp", "lat"),
        P("mp", "tp"),
        P(),
        P(),
        P(),
    )
    return jax.shard_map(
        local,
        mesh=mesh,
        in_specs=placed,
        out_specs=(P("mp", "tp", "lat"), P("mp", "tp", "lat")),
        check_vma=False,
    )
```

```python
import functools

import jax
import jax.numpy as jnp
from jax import lax
from jax.experimental import pallas as pl
from jax.experimental.pallas import tpu as pltpu
from jax.sharding import PartitionSpec as P

MESH = pl.DeviceIdType.MESH
f32, bf16 = jnp.float32, jnp.bfloat16
EPS = 1e-06
NB = 3
ROWS = 384
LAG = 0
R = ROWS // NB
RZ = R // 8
RX = R // 16
CW = 448
LW = 1024
HL = 512

LAST = (((1,), (1,)), ((), ()))
PLAIN = (((1,), (0,)), ((), ()))
FIRST = (((0,), (0,)), ((), ()))


def dot(a, b, dims=PLAIN):
    return lax.dot_general(a, b, dims, preferred_element_type=f32)


def merge(v, rows):
    return v.astype(f32).reshape(rows, v.shape[-1]).astype(bf16)


SCRATCH = {
    "payload": pltpu.VMEM((2, 12, 512), bf16),
    "own24": pltpu.VMEM((24, 512), f32),
    "nx": pltpu.VMEM((16, 24, 512), bf16),
    "xf": pltpu.VMEM((ROWS, 512), f32),
    "wgu": pltpu.VMEM((2 * CW, CW), bf16),
    "wrow": pltpu.VMEM((ROWS, 128), f32),
    "nsq": pltpu.VMEM((8, 1, LW), f32),
    "cn": pltpu.VMEM((2, 1, LW), f32),
    "pg": pltpu.VMEM((NB, 8, RZ, 2 * CW), bf16),
    "rg": pltpu.VMEM((NB, 8, RZ, 2 * CW), bf16),
    "hd": pltpu.VMEM((NB, 8, RZ, CW), bf16),
    "pm": pltpu.VMEM((2, NB, 16, RX, CW), bf16),
    "rm": pltpu.VMEM((2, NB, 16, RX, CW), bf16),
    "hs": pltpu.VMEM((2, NB, RX, CW), bf16),
    "hr": pltpu.VMEM((2, NB, RX, CW), bf16),
    "sq": pltpu.VMEM((NB, 8, RX, 128), f32),
    "rsd": pltpu.VMEM((NB, 16, RX, CW), bf16),
    "err": pltpu.VMEM((NB, 16, RX, CW), bf16),
    "ms": pltpu.VMEM((2, NB, R, HL), bf16),
    "mr": pltpu.VMEM((2, NB, R, HL), bf16),
    "pe": pltpu.VMEM((2, NB, 8, RZ, HL), bf16),
    "re": pltpu.VMEM((2, NB, 8, RZ, HL), bf16),
    "act": pltpu.VMEM((NB, RZ, HL), f32),
    "fe": pltpu.VMEM((NB, 2, 8, RZ, HL), bf16),
    "pd": pltpu.VMEM((NB, 2, 8, RZ, HL), bf16),
    "wd": pltpu.VMEM((CW, CW), bf16),
    "ew": pltpu.VMEM((CW, LW), bf16),
    "dw": pltpu.VMEM((CW, LW), bf16),
    "eg": pltpu.VMEM((CW, LW), bf16),
    "dg": pltpu.VMEM((CW, LW), bf16),
    "load": pltpu.SemaphoreType.DMA((8,)),
    "sem": pltpu.SemaphoreType.DMA((2, 200 * NB + 40)),
}


def kernel(*refs):
    (x_ref, pre_ref, wg_hbm, wu_hbm, wd_hbm, post_ref, ew_hbm, eb_ref, dw_hbm, db_ref,
     prompt_ref, pad_ref, ids_ref, eg_hbm, dg_hbm) = refs[:15]
    s = dict(zip(SCRATCH, refs[15:]))
    wd_ref, ew_ref, dw_ref, eg_ref, dg_ref = s["wd"], s["ew"], s["dw"], s["eg"], s["dg"]
    sem = s["sem"]
    m, i, lat = lax.axis_index("mp"), lax.axis_index("tp"), lax.axis_index("lat")
    q, h = lax.div(lat, 2), lax.rem(lat, 2)
    to_z = [{"tp": lax.rem(i + k, 8)} for k in range(1, 8)]
    to_q = [lax.rem(q + k, 16) for k in range(1, 16)]
    to_xy = [{"lat": 2 * p + h} for p in to_q]
    to_h = {"lat": 2 * q + 1 - h}
    to_m = {"mp": 1 - m}

    gate = pltpu.get_barrier_semaphore()
    everyone = to_z + to_xy + [to_h, to_m]
    for d in everyone:
        pl.semaphore_signal(gate, inc=1, device_id=d, device_id_type=MESH)

    def local_copy(src, dst, n):
        c = pltpu.make_async_copy(src, dst, s["load"].at[n])
        c.start()
        return c

    load_d = local_copy(dw_hbm.at[0], dw_ref, 0)
    load_g = [local_copy(wg_hbm.at[0], s["wgu"].at[pl.ds(0, CW)], 1),
              local_copy(wu_hbm.at[0], s["wgu"].at[pl.ds(CW, CW)], 2)]
    load_w = [local_copy(wd_hbm.at[0], wd_ref, 3), local_copy(ew_hbm.at[0], ew_ref, 4)]
    used, sends = [0], []

    def send(src, dst, where):
        n = used[0]
        used[0] += 1
        c = pltpu.make_async_remote_copy(
            src_ref=src, dst_ref=dst, send_sem=sem.at[0, n], recv_sem=sem.at[1, n],
            device_id=where, device_id_type=MESH)
        c.start()
        sends.append(c)
        return c

    def wait(copies):
        for c in copies:
            c.wait_recv()

    side, place = lax.div(i, 4), lax.rem(i, 4)
    mates = [lax.rem(place + k, 4) for k in range(1, 4)]
    to_mate = [{"tp": 4 * side + p} for p in mates]
    across = lax.rem(i + 4, 8)
    to_across = {"tp": across}

    def z_scatter(src, dst):
        far = [send(src.at[4 - 4 * side + p], dst.at[k], to_mate[k - 1]) for k, p in enumerate(mates, 1)]
        near = [send(src.at[4 * side + p], dst.at[4 + k], to_mate[k - 1]) for k, p in enumerate(mates, 1)]
        yield
        wait(far)
        src[across] = (src[across].astype(f32) + dst[1].astype(f32)
                       + dst[2].astype(f32) + dst[3].astype(f32)).astype(bf16)
        last = send(src.at[across], dst.at[4], to_across)
        yield
        wait(near + [last])

    def z_gather(ref):
        first = send(ref.at[i], ref.at[i], to_across)
        near = [send(ref.at[i], ref.at[i], d) for d in to_mate]
        yield
        wait([first])
        far = [send(ref.at[across], ref.at[across], d) for d in to_mate]
        yield
        wait(near + far)

    def z_share(ref):
        return [send(ref.at[i], ref.at[i], to_z[k - 1]) for k in range(1, 8)]

    def z_total(own, ref):
        acc = own.astype(f32)
        for k in range(4, 8):
            acc = acc + ref[k].astype(f32)
        return acc

    def xy_scatter(src, dst):
        return [send(src.at[to_q[k - 1]], dst.at[k], to_xy[k - 1]) for k in range(1, 16)]

    def xy_gather(ref):
        return [send(ref.at[q], ref.at[q], to_xy[k - 1]) for k in range(1, 16)]

    def total(own, ref, count):
        acc = own.astype(f32)
        for k in range(1, count):
            acc = acc + ref[k].astype(f32)
        return acc

    x = x_ref[0].astype(f32)
    scale = lax.rsqrt(jnp.sum(x * x, axis=1, keepdims=True) / (8 * CW) + EPS)
    p0 = scale.astype(bf16).astype(f32)
    p1 = (scale - p0).astype(bf16).astype(f32)
    p2 = scale - p0 - p1
    cols = jnp.zeros((12, CW), f32)
    gain_in = jnp.zeros((1, CW), f32)
    pre = pre_ref[...].astype(f32)
    for c in range(8):
        cols = jnp.where(i == c, x[:, c * CW:(c + 1) * CW], cols)
        gain_in = jnp.where(i == c, pre[:, c * CW:(c + 1) * CW], gain_in)
    payload = jnp.concatenate([cols, jnp.zeros((12, 64), f32)], axis=1)
    lane = lax.broadcasted_iota(jnp.int32, (12, 512), 1)
    payload = jnp.where(lane == CW, p0, jnp.where(lane == CW + 1, p1, jnp.where(lane == CW + 2, p2, payload)))
    s["payload"][h] = payload.astype(bf16)

    pl.semaphore_wait(gate, len(everyone))

    first = send(s["payload"].at[h], s["payload"].at[h], to_h)
    load_d.wait()
    dw = dw_ref[...].astype(f32)
    s["nsq"][i] = jnp.sum(dw * dw, axis=0, keepdims=True)
    wait([first])
    s["own24"][0:12] = s["payload"][0].astype(f32)
    s["own24"][12:24] = s["payload"][1].astype(f32)
    s["nx"][q] = s["own24"][...].astype(bf16)
    x_copies = xy_gather(s["nx"])
    norm_copies = z_share(s["nsq"])

    def column(v):
        return jnp.broadcast_to(v, (128, v.shape[1])).T[:, :1]

    prompt = column(prompt_ref[...])
    valid = column(pad_ref[...].astype(f32))
    in_prompt = prompt == lax.broadcasted_iota(jnp.int32, (ROWS, 96), 1)
    pair_of_prompt = lax.shift_right_logical(ids_ref[...], 1).astype(f32)
    pair = jnp.sum(jnp.where(in_prompt, pair_of_prompt, 0.0), axis=1, keepdims=True)
    in_pair = pair == lax.broadcasted_iota(jnp.int32, (ROWS, 48), 1).astype(f32)
    counts = jnp.sum(jnp.where(in_pair, valid, 0.0), axis=0, keepdims=True)
    inverse = 1.0 / jnp.maximum(counts, 1.0)
    wrow = valid * jnp.sum(jnp.where(in_pair, inverse, 0.0), axis=1, keepdims=True)
    s["wrow"][...] = jnp.broadcast_to(wrow, (ROWS, 128))

    post = post_ref[...].astype(f32)
    dbias = db_ref[...].astype(f32)
    half = pl.ds(pl.multiple_of(m * HL, HL), HL)
    other = pl.ds(pl.multiple_of((1 - m) * HL, HL), HL)

    for c in load_g + load_w:
        c.wait()
    wait(x_copies)
    s["xf"][...] = s["nx"][...].astype(f32).reshape(ROWS, 512)

    def mp_and_tp_sum(b, t, left, weight):
        s["ms"][t, b] = dot(left, weight[:, other]).astype(bf16)
        c = send(s["ms"].at[t, b], s["mr"].at[t, b], to_m)
        mine = dot(left, weight[:, half])
        c.wait_recv()
        both = mine + s["mr"][t, b].astype(f32)
        s["pe"][t, b] = both.reshape(8, RZ, HL).astype(bf16)
        yield from z_scatter(s["pe"].at[t, b], s["re"].at[t, b])

    def lat_sum(b, t, part):
        s["pm"][t, b] = part.reshape(16, RX, CW).astype(bf16)
        return xy_scatter(s["pm"].at[t, b], s["rm"].at[t, b])

    def block(b):
        rows = slice(b * R, (b + 1) * R)
        own_x = pl.ds(pl.multiple_of(b * R + q * RX, 8), RX)
        own_z = pl.ds(pl.multiple_of(b * R + i * RZ, 8), RZ)
        xb = s["xf"][rows]
        row_scale = xb[:, CW:CW + 1] + xb[:, CW + 1:CW + 2] + xb[:, CW + 2:CW + 3]
        normed = (xb[:, :CW] * row_scale * gain_in).astype(bf16)
        s["pg"][b] = dot(normed, s["wgu"][...], LAST).reshape(8, RZ, 2 * CW).astype(bf16)
        yield from z_scatter(s["pg"].at[b], s["rg"].at[b])
        both = z_total(s["pg"][b, i], s["rg"].at[b])
        g, u = both[:, :CW], both[:, CW:]
        s["hd"][b, i] = (0.5 * g * (1.0 + jnp.tanh(0.7978845608028654 * (g + 0.044715 * g * g * g))) * u).astype(bf16)
        yield from z_gather(s["hd"].at[b])
        c = lat_sum(b, 0, dot(merge(s["hd"][b], R), wd_ref[...]))
        yield
        wait(c)
        s["hs"][0, b] = total(s["pm"][0, b, q], s["rm"].at[0, b], 16).astype(bf16)
        c = [send(s["hs"].at[0, b], s["hr"].at[0, b], to_h)]
        yield
        wait(c)
        mixed = s["hs"][0, b].astype(f32) + s["hr"][0, b].astype(f32)
        s["sq"][b, i] = jnp.broadcast_to(jnp.sum(mixed * mixed, axis=1, keepdims=True), (RX, 128))
        c = z_share(s["sq"].at[b])
        yield
        wait(c)
        square = s["sq"][b, 0]
        for k in range(1, 8):
            square = square + s["sq"][b, k]
        out_scale = lax.rsqrt(square[:, :1] / (8 * CW) + EPS)
        s["rsd"][b, q] = (s["xf"][own_x, :][:, :CW] + mixed * out_scale * post).astype(bf16)
        c = xy_gather(s["rsd"].at[b])
        yield
        wait(c)
        yield from mp_and_tp_sum(b, 0, merge(s["rsd"][b], R), ew_ref)
        pre_act = z_total(s["pe"][0, b, i], s["re"].at[0, b]) + eb_ref[:, half].astype(f32)
        active = jnp.maximum(pre_act, 0.0)
        s["act"][b] = active
        s["fe"][b, m, i] = (active * active).astype(bf16)
        yield from z_gather(s["fe"].at[b, m])
        c = [send(s["fe"].at[b, m], s["fe"].at[b, m], to_m)]
        yield
        wait(c)
        recon = dot(merge(s["fe"][b, 0], R), dw_ref[:, :HL], LAST)
        recon = recon + dot(merge(s["fe"][b, 1], R), dw_ref[:, HL:], LAST)
        c = lat_sum(b, 1, recon)
        yield
        wait(c)
        s["hs"][1, b] = total(s["pm"][1, b, q], s["rm"].at[1, b], 16).astype(bf16)
        c = [send(s["hs"].at[1, b], s["hr"].at[1, b], to_h)]
        yield
        wait(c)
        error = s["hs"][1, b].astype(f32) + s["hr"][1, b].astype(f32) + dbias - s["rsd"][b, q].astype(f32)
        s["err"][b, q] = (2.0 * s["wrow"][own_x, :][:, :1] * error).astype(bf16)
        c = xy_gather(s["err"].at[b])
        yield
        wait(c)
        known.append(b)
        yield from mp_and_tp_sum(b, 1, merge(s["err"][b], R), dw_ref)
        norm_total = s["cn"][0, :, half] + s["cn"][1, :, half]
        grad = z_total(s["pe"][1, b, i], s["re"].at[1, b]) + s["wrow"][own_z, :][:, :1] * norm_total
        s["pd"][b, m, i] = (grad * 2.0 * s["act"][b]).astype(bf16)
        yield from z_gather(s["pd"].at[b, m])
        c = [send(s["pd"].at[b, m], s["pd"].at[b, m], to_m)]
        yield
        wait(c)

    out_copies = []
    known = []
    running = [(b, block(b)) for b in range(NB)]
    phase = 0
    while running:
        running = [(b, g) for b, g in running if phase < b * LAG or next(g, True) is None]
        phase += 1
        if phase == 2:
            wait(norm_copies)
            squares = s["nsq"][0]
            for k in range(1, 8):
                squares = squares + s["nsq"][k]
            s["cn"][m] = jnp.sqrt(squares + EPS)
            cn_copy = send(s["cn"].at[m], s["cn"].at[m], to_m)
        if phase == 3:
            cn_copy.wait_recv()
        if len(known) == NB:
            known.append(NB)
            err = merge(s["err"][...], ROWS)
            own_norm = s["cn"][m]
            for p in range(2):
                at = slice(p * HL, (p + 1) * HL)
                feats = s["fe"][:, p].astype(f32).reshape(ROWS, HL)
                weighted = jnp.sum(s["wrow"][:, :1] * feats, axis=0, keepdims=True)
                direct = dot(err, feats.astype(bf16), FIRST)
                dg_ref[:, at] = (
                    direct + weighted * dw_ref[:, at].astype(f32) / own_norm[:, at]).astype(bf16)
            out_copies.append(local_copy(dg_ref, dg_hbm.at[0], 5))

    resid = merge(s["rsd"][...], ROWS)
    for p in range(2):
        at = slice(p * HL, (p + 1) * HL)
        eg_ref[:, at] = dot(resid, merge(s["pd"][:, p], ROWS), FIRST).astype(bf16)
        out_copies.append(local_copy(eg_ref.at[:, at], eg_hbm.at[0, :, at], 6 + p))
    for c in sends:
        c.wait_send()
    for c in out_copies:
        c.wait()


def local(*args):
    args = list(args)
    for n in (7, 10, 11, 12):
        args[n] = args[n][None]
    vmem = pl.BlockSpec(memory_space=pltpu.VMEM)
    any_ = pl.BlockSpec(memory_space=pl.ANY)
    out = jax.ShapeDtypeStruct((1, CW, LW), bf16)
    return pl.pallas_call(
        kernel,
        out_shape=(out, out),
        in_specs=[any_ if n in (2, 3, 4, 6, 8) else vmem for n in range(13)],
        out_specs=(any_, any_),
        scratch_shapes=list(SCRATCH.values()),
        compiler_params=pltpu.CompilerParams(
            collective_id=1, has_side_effects=True, vmem_limit_bytes=56 << 20),
        cost_estimate=pl.CostEstimate(flops=2300000000, bytes_accessed=7000000, transcendentals=100000),
    )(*args)


def solution(mesh):
    placed = (
        P("mp", "lat", None),
        P("mp", None),
        P("mp", "lat", "tp"),
        P("mp", "lat", "tp"),
        P("mp", "lat", "tp"),
        P("mp", "tp"),
        P("mp", "tp", "lat"),
        P("lat"),
        P("mp", "tp", "lat"),
        P("mp", "tp"),
        P(),
        P(),
        P(),
    )
    return jax.shard_map(
        local,
        mesh=mesh,
        in_specs=placed,
        out_specs=(P("mp", "tp", "lat"), P("mp", "tp", "lat")),
        check_vma=False,
    )
```

```python
import functools

import jax
import jax.numpy as jnp
from jax import lax
from jax.experimental import pallas as pl
from jax.experimental.pallas import tpu as pltpu
from jax.sharding import PartitionSpec as P

MESH = pl.DeviceIdType.MESH
f32, bf16 = jnp.float32, jnp.bfloat16
EPS = 1e-06
NB = 3
ROWS = 384
R = ROWS // NB
RZ = R // 8
RX = R // 16
CW = 448
LW = 1024
HL = 512

LAST = (((1,), (1,)), ((), ()))
PLAIN = (((1,), (0,)), ((), ()))
FIRST = (((0,), (0,)), ((), ()))


def dot(a, b, dims=PLAIN):
    return lax.dot_general(a, b, dims, preferred_element_type=f32)


def merge(v, rows):
    return v.astype(f32).reshape(rows, v.shape[-1]).astype(bf16)


SCRATCH = {
    "payload": pltpu.VMEM((2, 12, 512), bf16),
    "own24": pltpu.VMEM((24, 512), f32),
    "nx": pltpu.VMEM((16, 24, 512), bf16),
    "xf": pltpu.VMEM((ROWS, 512), f32),
    "wgu": pltpu.VMEM((2 * CW, CW), bf16),
    "wrow": pltpu.VMEM((ROWS, 128), f32),
    "nsq": pltpu.VMEM((8, 1, LW), f32),
    "cn": pltpu.VMEM((2, 1, LW), f32),
    "pg": pltpu.VMEM((NB, 8, RZ, 2 * CW), bf16),
    "rg": pltpu.VMEM((NB, 8, RZ, 2 * CW), bf16),
    "hd": pltpu.VMEM((NB, 8, RZ, CW), bf16),
    "pm": pltpu.VMEM((2, NB, 16, RX, CW), bf16),
    "rm": pltpu.VMEM((2, NB, 16, RX, CW), bf16),
    "hs": pltpu.VMEM((2, NB, RX, CW), bf16),
    "hr": pltpu.VMEM((2, NB, RX, CW), bf16),
    "sq": pltpu.VMEM((NB, 8, RX, 128), f32),
    "rsd": pltpu.VMEM((NB, 16, RX, CW), bf16),
    "err": pltpu.VMEM((NB, 16, RX, CW), bf16),
    "ms": pltpu.VMEM((2, NB, R, HL), bf16),
    "mr": pltpu.VMEM((2, NB, R, HL), bf16),
    "pe": pltpu.VMEM((2, NB, 8, RZ, HL), bf16),
    "re": pltpu.VMEM((2, NB, 8, RZ, HL), bf16),
    "act": pltpu.VMEM((NB, RZ, HL), f32),
    "fe": pltpu.VMEM((NB, 2, 8, RZ, HL), bf16),
    "pd": pltpu.VMEM((NB, 2, 8, RZ, HL), bf16),
    "wd": pltpu.VMEM((CW, CW), bf16),
    "ew": pltpu.VMEM((CW, LW), bf16),
    "dw": pltpu.VMEM((CW, LW), bf16),
    "eg": pltpu.VMEM((CW, LW), bf16),
    "dg": pltpu.VMEM((CW, LW), bf16),
    "eb": pltpu.VMEM((1, LW), f32),
    "load": pltpu.SemaphoreType.DMA((8,)),
    "sem": pltpu.SemaphoreType.DMA((2, 32 * NB + 4)),
}


def kernel(*refs):
    (x_ref, pre_ref, wg_hbm, wu_hbm, wd_hbm, post_ref, ew_hbm, eb_ref, dw_hbm, db_ref,
     prompt_ref, pad_ref, ids_ref, eg_hbm, dg_hbm) = refs[:15]
    s = dict(zip(SCRATCH, refs[15:]))
    wd_ref, ew_ref, dw_ref, eg_ref, dg_ref = s["wd"], s["ew"], s["dw"], s["eg"], s["dg"]
    sem = s["sem"]
    m, i, lat = lax.axis_index("mp"), lax.axis_index("tp"), lax.axis_index("lat")
    q, h = lax.div(lat, 2), lax.rem(lat, 2)
    to_z = [{"tp": lax.rem(i + k, 8)} for k in range(1, 8)]
    to_q = [lax.rem(q + k, 16) for k in range(1, 16)]
    to_xy = [{"lat": 2 * p + h} for p in to_q]
    to_h = {"lat": 2 * q + 1 - h}
    to_m = {"mp": 1 - m}

    gate = pltpu.get_barrier_semaphore()
    everyone = to_z + to_xy + [to_h, to_m]
    for d in everyone:
        pl.semaphore_signal(gate, inc=1, device_id=d, device_id_type=MESH)

    def local_copy(src, dst, n):
        c = pltpu.make_async_copy(src, dst, s["load"].at[n])
        c.start()
        return c

    load_d = local_copy(dw_hbm.at[0], dw_ref, 0)
    load_g = [local_copy(wg_hbm.at[0], s["wgu"].at[pl.ds(0, CW)], 1),
              local_copy(wu_hbm.at[0], s["wgu"].at[pl.ds(CW, CW)], 2)]
    load_w = [local_copy(wd_hbm.at[0], wd_ref, 3), local_copy(ew_hbm.at[0], ew_ref, 4)]
    used, sends = [0], []

    def link(n, src, dst, where):
        return pltpu.make_async_remote_copy(
            src_ref=src, dst_ref=dst, send_sem=sem.at[0, n], recv_sem=sem.at[1, n],
            device_id=where, device_id_type=MESH)

    def send(copies, whole):
        n = used[0]
        used[0] += 1
        for src, dst, where in copies:
            link(n, src, dst, where).start()
        sends.append(link(n, whole, whole, to_m))
        return sends[-1]

    def wait(*groups):
        for c in groups:
            c.wait_recv()

    side, place = lax.div(i, 4), lax.rem(i, 4)
    mates = [lax.rem(place + k, 4) for k in range(1, 4)]
    to_mate = [{"tp": 4 * side + p} for p in mates]
    across = lax.rem(i + 4, 8)
    to_across = {"tp": across}

    def z_scatter(src, dst):
        far = send([(src.at[4 - 4 * side + p], dst.at[k], to_mate[k - 1])
                    for k, p in enumerate(mates, 1)], dst.at[pl.ds(1, 3)])
        near = send([(src.at[4 * side + p], dst.at[4 + k], to_mate[k - 1])
                     for k, p in enumerate(mates, 1)], dst.at[pl.ds(5, 3)])
        yield
        wait(far)
        src[across] = (src[across].astype(f32) + dst[1].astype(f32)
                       + dst[2].astype(f32) + dst[3].astype(f32)).astype(bf16)
        last = send([(src.at[across], dst.at[4], to_across)], dst.at[4])
        yield
        wait(near, last)

    def z_gather(ref):
        first = send([(ref.at[i], ref.at[i], to_across)], ref.at[0])
        near = send([(ref.at[i], ref.at[i], d) for d in to_mate], ref.at[pl.ds(0, 3)])
        yield
        wait(first)
        far = send([(ref.at[across], ref.at[across], d) for d in to_mate], ref.at[pl.ds(0, 3)])
        yield
        wait(near, far)

    def z_share(ref):
        return send([(ref.at[i], ref.at[i], d) for d in to_z], ref.at[pl.ds(0, 7)])

    def z_total(own, ref):
        acc = own.astype(f32)
        for k in range(4, 8):
            acc = acc + ref[k].astype(f32)
        return acc

    def xy_scatter(src, dst):
        return send([(src.at[to_q[k - 1]], dst.at[k], to_xy[k - 1]) for k in range(1, 16)],
                    dst.at[pl.ds(1, 15)])

    def xy_gather(ref):
        return send([(ref.at[q], ref.at[q], d) for d in to_xy], ref.at[pl.ds(0, 15)])

    def total(own, ref, count):
        acc = own.astype(f32)
        for k in range(1, count):
            acc = acc + ref[k].astype(f32)
        return acc

    x = x_ref[0].astype(f32)
    scale = lax.rsqrt(jnp.sum(x * x, axis=1, keepdims=True) / (8 * CW) + EPS)
    p0 = scale.astype(bf16).astype(f32)
    p1 = (scale - p0).astype(bf16).astype(f32)
    p2 = scale - p0 - p1
    cols = jnp.zeros((12, CW), f32)
    gain_in = jnp.zeros((1, CW), f32)
    pre = pre_ref[...].astype(f32)
    for c in range(8):
        cols = jnp.where(i == c, x[:, c * CW:(c + 1) * CW], cols)
        gain_in = jnp.where(i == c, pre[:, c * CW:(c + 1) * CW], gain_in)
    payload = jnp.concatenate([cols, jnp.zeros((12, 64), f32)], axis=1)
    lane = lax.broadcasted_iota(jnp.int32, (12, 512), 1)
    payload = jnp.where(lane == CW, p0, jnp.where(lane == CW + 1, p1, jnp.where(lane == CW + 2, p2, payload)))
    s["payload"][h] = payload.astype(bf16)

    pl.semaphore_wait(gate, len(everyone))

    first = send([(s["payload"].at[h], s["payload"].at[h], to_h)], s["payload"].at[0])
    load_d.wait()
    dw = dw_ref[...].astype(f32)
    s["nsq"][i] = jnp.sum(dw * dw, axis=0, keepdims=True)
    wait(first)
    s["own24"][0:12] = s["payload"][0].astype(f32)
    s["own24"][12:24] = s["payload"][1].astype(f32)
    s["nx"][q] = s["own24"][...].astype(bf16)
    x_copies = xy_gather(s["nx"])
    norm_copies = z_share(s["nsq"])

    def column(v):
        return jnp.broadcast_to(v, (128, v.shape[1])).T[:, :1]

    prompt = column(prompt_ref[...].reshape(1, ROWS))
    valid = column(pad_ref[...].reshape(1, ROWS).astype(f32))
    in_prompt = prompt == lax.broadcasted_iota(jnp.int32, (ROWS, 96), 1)
    pair_of_prompt = lax.shift_right_logical(ids_ref[...].reshape(1, 96), 1).astype(f32)
    pair = jnp.sum(jnp.where(in_prompt, pair_of_prompt, 0.0), axis=1, keepdims=True)
    in_pair = pair == lax.broadcasted_iota(jnp.int32, (ROWS, 48), 1).astype(f32)
    counts = jnp.sum(jnp.where(in_pair, valid, 0.0), axis=0, keepdims=True)
    inverse = 1.0 / jnp.maximum(counts, 1.0)
    wrow = valid * jnp.sum(jnp.where(in_pair, inverse, 0.0), axis=1, keepdims=True)
    s["wrow"][...] = jnp.broadcast_to(wrow, (ROWS, 128))

    s["eb"][...] = eb_ref[...].astype(f32).reshape(1, LW)
    post = post_ref[...].astype(f32)
    dbias = db_ref[...].astype(f32)
    half = pl.ds(pl.multiple_of(m * HL, HL), HL)
    other = pl.ds(pl.multiple_of((1 - m) * HL, HL), HL)

    for c in load_g + load_w:
        c.wait()
    wait(x_copies)
    s["xf"][...] = s["nx"][...].astype(f32).reshape(ROWS, 512)

    def mp_and_tp_sum(b, t, left, weight):
        s["ms"][t, b] = dot(left, weight[:, other]).astype(bf16)
        c = send([(s["ms"].at[t, b], s["mr"].at[t, b], to_m)], s["mr"].at[t, b])
        mine = dot(left, weight[:, half])
        c.wait_recv()
        both = mine + s["mr"][t, b].astype(f32)
        s["pe"][t, b] = both.reshape(8, RZ, HL).astype(bf16)
        yield from z_scatter(s["pe"].at[t, b], s["re"].at[t, b])

    def lat_sum(b, t, part):
        s["pm"][t, b] = part.reshape(16, RX, CW).astype(bf16)
        return xy_scatter(s["pm"].at[t, b], s["rm"].at[t, b])

    def block(b):
        rows = slice(b * R, (b + 1) * R)
        own_x = pl.ds(pl.multiple_of(b * R + q * RX, 8), RX)
        own_z = pl.ds(pl.multiple_of(b * R + i * RZ, 8), RZ)
        xb = s["xf"][rows]
        row_scale = xb[:, CW:CW + 1] + xb[:, CW + 1:CW + 2] + xb[:, CW + 2:CW + 3]
        normed = (xb[:, :CW] * row_scale * gain_in).astype(bf16)
        s["pg"][b] = dot(normed, s["wgu"][...], LAST).reshape(8, RZ, 2 * CW).astype(bf16)
        yield from z_scatter(s["pg"].at[b], s["rg"].at[b])
        both = z_total(s["pg"][b, i], s["rg"].at[b])
        g, u = both[:, :CW], both[:, CW:]
        s["hd"][b, i] = (0.5 * g * (1.0 + jnp.tanh(0.7978845608028654 * (g + 0.044715 * g * g * g))) * u).astype(bf16)
        yield from z_gather(s["hd"].at[b])
        c = lat_sum(b, 0, dot(merge(s["hd"][b], R), wd_ref[...]))
        yield
        wait(c)
        s["hs"][0, b] = total(s["pm"][0, b, q], s["rm"].at[0, b], 16).astype(bf16)
        c = send([(s["hs"].at[0, b], s["hr"].at[0, b], to_h)], s["hr"].at[0, b])
        yield
        wait(c)
        mixed = s["hs"][0, b].astype(f32) + s["hr"][0, b].astype(f32)
        s["sq"][b, i] = jnp.broadcast_to(jnp.sum(mixed * mixed, axis=1, keepdims=True), (RX, 128))
        c = z_share(s["sq"].at[b])
        yield
        wait(c)
        square = s["sq"][b, 0]
        for k in range(1, 8):
            square = square + s["sq"][b, k]
        out_scale = lax.rsqrt(square[:, :1] / (8 * CW) + EPS)
        s["rsd"][b, q] = (s["xf"][own_x, :][:, :CW] + mixed * out_scale * post).astype(bf16)
        c = xy_gather(s["rsd"].at[b])
        yield
        wait(c)
        yield from mp_and_tp_sum(b, 0, merge(s["rsd"][b], R), ew_ref)
        pre_act = z_total(s["pe"][0, b, i], s["re"].at[0, b]) + s["eb"][:, half]
        active = jnp.maximum(pre_act, 0.0)
        s["act"][b] = active
        s["fe"][b, m, i] = (active * active).astype(bf16)
        yield from z_gather(s["fe"].at[b, m])
        c = send([(s["fe"].at[b, m], s["fe"].at[b, m], to_m)], s["fe"].at[b, 0])
        yield
        wait(c)
        recon = dot(merge(s["fe"][b, 0], R), dw_ref[:, :HL], LAST)
        recon = recon + dot(merge(s["fe"][b, 1], R), dw_ref[:, HL:], LAST)
        c = lat_sum(b, 1, recon)
        yield
        wait(c)
        s["hs"][1, b] = total(s["pm"][1, b, q], s["rm"].at[1, b], 16).astype(bf16)
        c = send([(s["hs"].at[1, b], s["hr"].at[1, b], to_h)], s["hr"].at[1, b])
        yield
        wait(c)
        error = s["hs"][1, b].astype(f32) + s["hr"][1, b].astype(f32) + dbias - s["rsd"][b, q].astype(f32)
        s["err"][b, q] = (2.0 * s["wrow"][own_x, :][:, :1] * error).astype(bf16)
        c = xy_gather(s["err"].at[b])
        yield
        wait(c)
        known.append(b)
        yield from mp_and_tp_sum(b, 1, merge(s["err"][b], R), dw_ref)
        norm_total = s["cn"][0, :, half] + s["cn"][1, :, half]
        grad = z_total(s["pe"][1, b, i], s["re"].at[1, b]) + s["wrow"][own_z, :][:, :1] * norm_total
        s["pd"][b, m, i] = (grad * 2.0 * s["act"][b]).astype(bf16)
        yield from z_gather(s["pd"].at[b, m])
        c = send([(s["pd"].at[b, m], s["pd"].at[b, m], to_m)], s["pd"].at[b, 0])
        yield
        wait(c)

    out_copies = []
    known = []
    running = [(b, block(b)) for b in range(NB)]
    phase = 0
    while running:
        running = [(b, g) for b, g in running if next(g, True) is None]
        phase += 1
        if phase == 2:
            wait(norm_copies)
            squares = s["nsq"][0]
            for k in range(1, 8):
                squares = squares + s["nsq"][k]
            s["cn"][m] = jnp.sqrt(squares + EPS)
            cn_copy = send([(s["cn"].at[m], s["cn"].at[m], to_m)], s["cn"].at[0])
        if phase == 3:
            cn_copy.wait_recv()
        if len(known) == NB:
            known.append(NB)
            err = merge(s["err"][...], ROWS)
            own_norm = s["cn"][m]
            for p in range(2):
                at = slice(p * HL, (p + 1) * HL)
                feats = s["fe"][:, p].astype(f32).reshape(ROWS, HL)
                weighted = jnp.sum(s["wrow"][:, :1] * feats, axis=0, keepdims=True)
                direct = dot(err, feats.astype(bf16), FIRST)
                dg_ref[:, at] = (
                    direct + weighted * dw_ref[:, at].astype(f32) / own_norm[:, at]).astype(bf16)
            out_copies.append(local_copy(dg_ref, dg_hbm.at[0], 5))

    resid = merge(s["rsd"][...], ROWS)
    for p in range(2):
        at = slice(p * HL, (p + 1) * HL)
        eg_ref[:, at] = dot(resid, merge(s["pd"][:, p], ROWS), FIRST).astype(bf16)
        out_copies.append(local_copy(eg_ref.at[:, at], eg_hbm.at[0, :, at], 6 + p))
    for c in sends:
        c.wait_send()
    for c in out_copies:
        c.wait()


def local(*args):
    vmem = pl.BlockSpec(memory_space=pltpu.VMEM)
    any_ = pl.BlockSpec(memory_space=pl.ANY)
    out = jax.ShapeDtypeStruct((1, CW, LW), bf16)
    return pl.pallas_call(
        kernel,
        out_shape=(out, out),
        in_specs=[any_ if n in (2, 3, 4, 6, 8) else vmem for n in range(13)],
        out_specs=(any_, any_),
        scratch_shapes=list(SCRATCH.values()),
        compiler_params=pltpu.CompilerParams(
            collective_id=1, has_side_effects=True, vmem_limit_bytes=56 << 20),
        cost_estimate=pl.CostEstimate(flops=2300000000, bytes_accessed=7000000, transcendentals=100000),
    )(*args)


def solution(mesh):
    placed = (
        P("mp", "lat", None),
        P("mp", None),
        P("mp", "lat", "tp"),
        P("mp", "lat", "tp"),
        P("mp", "lat", "tp"),
        P("mp", "tp"),
        P("mp", "tp", "lat"),
        P("lat"),
        P("mp", "tp", "lat"),
        P("mp", "tp"),
        P(),
        P(),
        P(),
    )
    return jax.shard_map(
        local,
        mesh=mesh,
        in_specs=placed,
        out_specs=(P("mp", "tp", "lat"), P("mp", "tp", "lat")),
        check_vma=False,
    )
```

```python
import functools

import jax
import jax.numpy as jnp
from jax import lax
from jax.experimental import pallas as pl
from jax.experimental.pallas import tpu as pltpu
from jax.sharding import PartitionSpec as P

MESH = pl.DeviceIdType.MESH
f32, bf16 = jnp.float32, jnp.bfloat16
EPS = 1e-06
NB = 3
ROWS = 384
R = ROWS // NB
RZ = R // 8
RX = R // 16
CW = 448
LW = 1024
HL = 512

LAST = (((1,), (1,)), ((), ()))
PLAIN = (((1,), (0,)), ((), ()))
FIRST = (((0,), (0,)), ((), ()))


def dot(a, b, dims=PLAIN):
    return lax.dot_general(a, b, dims, preferred_element_type=f32)


def merge(v, rows):
    return v.astype(f32).reshape(rows, v.shape[-1]).astype(bf16)


SCRATCH = {
    "edge": pltpu.VMEM((4, 12, 512), bf16),
    "nx": pltpu.VMEM((2, 16, 12, 512), bf16),
    "xf": pltpu.VMEM((ROWS, 512), f32),
    "wgu": pltpu.VMEM((2 * CW, CW), bf16),
    "wrow": pltpu.VMEM((ROWS, 128), f32),
    "nsq": pltpu.VMEM((8, 1, LW), f32),
    "cn": pltpu.VMEM((2, 1, LW), f32),
    "pg": pltpu.VMEM((NB, 8, RZ, 2 * CW), bf16),
    "rg": pltpu.VMEM((NB, 8, RZ, 2 * CW), bf16),
    "hd": pltpu.VMEM((NB, 8, RZ, CW), bf16),
    "pm": pltpu.VMEM((2, NB, 16, RX, CW), bf16),
    "rm": pltpu.VMEM((2, NB, 16, RX, CW), bf16),
    "hs": pltpu.VMEM((2, NB, RX, CW), bf16),
    "hr": pltpu.VMEM((2, NB, RX, CW), bf16),
    "sq": pltpu.VMEM((NB, 8, RX, 128), f32),
    "rsd": pltpu.VMEM((NB, 16, RX, CW), bf16),
    "err": pltpu.VMEM((NB, 16, RX, CW), bf16),
    "ms": pltpu.VMEM((2, NB, R, HL), bf16),
    "mr": pltpu.VMEM((2, NB, R, HL), bf16),
    "pe": pltpu.VMEM((2, NB, 8, RZ, HL), bf16),
    "re": pltpu.VMEM((2, NB, 8, RZ, HL), bf16),
    "act": pltpu.VMEM((NB, RZ, HL), f32),
    "fe": pltpu.VMEM((NB, 2, 8, RZ, HL), bf16),
    "pd": pltpu.VMEM((NB, 2, 8, RZ, HL), bf16),
    "wd": pltpu.VMEM((CW, CW), bf16),
    "ew": pltpu.VMEM((CW, LW), bf16),
    "dw": pltpu.VMEM((CW, LW), bf16),
    "eg": pltpu.VMEM((CW, LW), bf16),
    "dg": pltpu.VMEM((CW, LW), bf16),
    "eb": pltpu.VMEM((1, LW), f32),
    "load": pltpu.SemaphoreType.DMA((8,)),
    "sem": pltpu.SemaphoreType.DMA((2, 32 * NB + 6)),
}


def kernel(*refs):
    (x_ref, pre_ref, wg_hbm, wu_hbm, wd_hbm, post_ref, ew_hbm, eb_ref, dw_hbm, db_ref,
     prompt_ref, pad_ref, ids_ref, eg_hbm, dg_hbm) = refs[:15]
    s = dict(zip(SCRATCH, refs[15:]))
    wd_ref, ew_ref, dw_ref, eg_ref, dg_ref = s["wd"], s["ew"], s["dw"], s["eg"], s["dg"]
    sem = s["sem"]
    m, i, lat = lax.axis_index("mp"), lax.axis_index("tp"), lax.axis_index("lat")
    q, h = lax.div(lat, 2), lax.rem(lat, 2)
    to_z = [{"tp": lax.rem(i + k, 8)} for k in range(1, 8)]
    to_q = [lax.rem(q + k, 16) for k in range(1, 16)]
    to_xy = [{"lat": 2 * p + h} for p in to_q]
    to_h = {"lat": 2 * q + 1 - h}
    to_m = {"mp": 1 - m}

    gate = pltpu.get_barrier_semaphore()
    other_lat = 2 * q + 1 - h
    nearest = {"tp": jnp.where(i < 4, 7, 0), "lat": other_lat}
    at_edge = jnp.logical_or(i == 0, i == 7)
    everyone = to_z + to_xy + [to_h, to_m, nearest]
    for d in everyone:
        pl.semaphore_signal(gate, inc=1, device_id=d, device_id_type=MESH)

    def local_copy(src, dst, n):
        c = pltpu.make_async_copy(src, dst, s["load"].at[n])
        c.start()
        return c

    load_d = local_copy(dw_hbm.at[0], dw_ref, 0)
    load_g = [local_copy(wg_hbm.at[0], s["wgu"].at[pl.ds(0, CW)], 1),
              local_copy(wu_hbm.at[0], s["wgu"].at[pl.ds(CW, CW)], 2)]
    load_w = [local_copy(wd_hbm.at[0], wd_ref, 3), local_copy(ew_hbm.at[0], ew_ref, 4)]
    used, sends = [0], []

    def link(n, src, dst, where):
        return pltpu.make_async_remote_copy(
            src_ref=src, dst_ref=dst, send_sem=sem.at[0, n], recv_sem=sem.at[1, n],
            device_id=where, device_id_type=MESH)

    def send(copies, whole):
        n = used[0]
        used[0] += 1
        for src, dst, where in copies:
            link(n, src, dst, where).start()
        sends.append(link(n, whole, whole, to_m))
        return sends[-1]

    def wait(*groups):
        for c in groups:
            c.wait_recv()

    side, place = lax.div(i, 4), lax.rem(i, 4)
    mates = [lax.rem(place + k, 4) for k in range(1, 4)]
    to_mate = [{"tp": 4 * side + p} for p in mates]
    across = lax.rem(i + 4, 8)
    to_across = {"tp": across}

    def z_scatter(src, dst):
        far = send([(src.at[4 - 4 * side + p], dst.at[k], to_mate[k - 1])
                    for k, p in enumerate(mates, 1)], dst.at[pl.ds(1, 3)])
        yield
        wait(far)
        src[across] = (src[across].astype(f32) + dst[1].astype(f32)
                       + dst[2].astype(f32) + dst[3].astype(f32)).astype(bf16)
        last = send([(src.at[across], dst.at[4], to_across)], dst.at[4])
        near = send([(src.at[4 * side + p], dst.at[4 + k], to_mate[k - 1])
                     for k, p in enumerate(mates, 1)], dst.at[pl.ds(5, 3)])
        yield
        wait(near, last)

    def z_gather(ref):
        first = send([(ref.at[i], ref.at[i], to_across)], ref.at[0])
        near = send([(ref.at[i], ref.at[i], d) for d in to_mate], ref.at[pl.ds(0, 3)])
        yield
        wait(first)
        far = send([(ref.at[across], ref.at[across], d) for d in to_mate], ref.at[pl.ds(0, 3)])
        yield
        wait(near, far)

    def z_share(ref):
        return send([(ref.at[i], ref.at[i], d) for d in to_z], ref.at[pl.ds(0, 7)])

    def z_total(own, ref):
        acc = own.astype(f32)
        for k in range(4, 8):
            acc = acc + ref[k].astype(f32)
        return acc

    def xy_scatter(src, dst):
        return send([(src.at[to_q[k - 1]], dst.at[k], to_xy[k - 1]) for k in range(1, 16)],
                    dst.at[pl.ds(1, 15)])

    def xy_gather(ref):
        return send([(ref.at[q], ref.at[q], d) for d in to_xy], ref.at[pl.ds(0, 15)])

    def total(own, ref, count):
        acc = own.astype(f32)
        for k in range(1, count):
            acc = acc + ref[k].astype(f32)
        return acc

    x = x_ref[0].astype(f32)
    scale = lax.rsqrt(jnp.sum(x * x, axis=1, keepdims=True) / (8 * CW) + EPS)
    p0 = scale.astype(bf16).astype(f32)
    p1 = (scale - p0).astype(bf16).astype(f32)
    p2 = scale - p0 - p1
    lane = lax.broadcasted_iota(jnp.int32, (12, 512), 1)

    def payload(cols):
        wide = jnp.concatenate([cols, jnp.zeros((12, 64), f32)], axis=1)
        wide = jnp.where(lane == CW, p0, jnp.where(lane == CW + 1, p1, jnp.where(lane == CW + 2, p2, wide)))
        return wide.astype(bf16)

    cols = jnp.zeros((12, CW), f32)
    gain_in = jnp.zeros((1, CW), f32)
    pre = pre_ref[...].astype(f32)
    for c in range(8):
        cols = jnp.where(i == c, x[:, c * CW:(c + 1) * CW], cols)
        gain_in = jnp.where(i == c, pre[:, c * CW:(c + 1) * CW], gain_in)
    s["nx"][h, q] = payload(cols)
    for edge, low in ((7, 0), (0, 4)):
        @pl.when(i == edge)
        def _():
            for c in range(4):
                s["edge"][c] = payload(x[:, (low + c) * CW:(low + c + 1) * CW])

    pl.semaphore_wait(gate, jnp.where(at_edge, len(everyone) + 3, len(everyone) - 1))

    edge_n = used[0]
    used[0] += 1
    for edge, low in ((7, 0), (0, 4)):
        @pl.when(i == edge)
        def _():
            for c in range(4):
                link(edge_n, s["edge"].at[c], s["nx"].at[h, q], {"tp": low + c, "lat": other_lat}).start()

    def rows_gather(part):
        return send([(part.at[q], part.at[q], d) for d in to_xy], part.at[pl.ds(0, 15)])

    own_copies = rows_gather(s["nx"].at[h])
    load_d.wait()
    dw = dw_ref[...].astype(f32)
    s["nsq"][i] = jnp.sum(dw * dw, axis=0, keepdims=True)
    link(edge_n, s["nx"].at[0, 0], s["nx"].at[0, 0], to_m).wait_recv()
    other_copies = rows_gather(s["nx"].at[1 - h])
    norm_copies = z_share(s["nsq"])

    def column(v):
        return jnp.broadcast_to(v, (128, v.shape[1])).T[:, :1]

    prompt = column(prompt_ref[...].reshape(1, ROWS))
    valid = column(pad_ref[...].reshape(1, ROWS).astype(f32))
    in_prompt = prompt == lax.broadcasted_iota(jnp.int32, (ROWS, 96), 1)
    pair_of_prompt = lax.shift_right_logical(ids_ref[...].reshape(1, 96), 1).astype(f32)
    pair = jnp.sum(jnp.where(in_prompt, pair_of_prompt, 0.0), axis=1, keepdims=True)
    in_pair = pair == lax.broadcasted_iota(jnp.int32, (ROWS, 48), 1).astype(f32)
    counts = jnp.sum(jnp.where(in_pair, valid, 0.0), axis=0, keepdims=True)
    inverse = 1.0 / jnp.maximum(counts, 1.0)
    wrow = valid * jnp.sum(jnp.where(in_pair, inverse, 0.0), axis=1, keepdims=True)
    s["wrow"][...] = jnp.broadcast_to(wrow, (ROWS, 128))

    s["eb"][...] = eb_ref[...].astype(f32).reshape(1, LW)
    post = post_ref[...].astype(f32)
    dbias = db_ref[...].astype(f32)
    half = pl.ds(pl.multiple_of(m * HL, HL), HL)
    other = pl.ds(pl.multiple_of((1 - m) * HL, HL), HL)

    for c in load_g + load_w:
        c.wait()
    wait(own_copies, other_copies)
    for c in range(32):
        s["xf"][12 * c:12 * (c + 1)] = s["nx"][c % 2, c // 2].astype(f32)

    def mp_and_tp_sum(b, t, left, weight):
        s["ms"][t, b] = dot(left, weight[:, other]).astype(bf16)
        c = send([(s["ms"].at[t, b], s["mr"].at[t, b], to_m)], s["mr"].at[t, b])
        mine = dot(left, weight[:, half])
        c.wait_recv()
        both = mine + s["mr"][t, b].astype(f32)
        s["pe"][t, b] = both.reshape(8, RZ, HL).astype(bf16)
        yield from z_scatter(s["pe"].at[t, b], s["re"].at[t, b])

    def lat_sum(b, t, part):
        s["pm"][t, b] = part.reshape(16, RX, CW).astype(bf16)
        return xy_scatter(s["pm"].at[t, b], s["rm"].at[t, b])

    def block(b):
        rows = slice(b * R, (b + 1) * R)
        own_x = pl.ds(pl.multiple_of(b * R + q * RX, 8), RX)
        own_z = pl.ds(pl.multiple_of(b * R + i * RZ, 8), RZ)
        xb = s["xf"][rows]
        row_scale = xb[:, CW:CW + 1] + xb[:, CW + 1:CW + 2] + xb[:, CW + 2:CW + 3]
        normed = (xb[:, :CW] * row_scale * gain_in).astype(bf16)
        s["pg"][b] = dot(normed, s["wgu"][...], LAST).reshape(8, RZ, 2 * CW).astype(bf16)
        yield from z_scatter(s["pg"].at[b], s["rg"].at[b])
        both = z_total(s["pg"][b, i], s["rg"].at[b])
        g, u = both[:, :CW], both[:, CW:]
        s["hd"][b, i] = (0.5 * g * (1.0 + jnp.tanh(0.7978845608028654 * (g + 0.044715 * g * g * g))) * u).astype(bf16)
        yield from z_gather(s["hd"].at[b])
        c = lat_sum(b, 0, dot(merge(s["hd"][b], R), wd_ref[...]))
        yield
        wait(c)
        s["hs"][0, b] = total(s["pm"][0, b, q], s["rm"].at[0, b], 16).astype(bf16)
        c = send([(s["hs"].at[0, b], s["hr"].at[0, b], to_h)], s["hr"].at[0, b])
        yield
        wait(c)
        mixed = s["hs"][0, b].astype(f32) + s["hr"][0, b].astype(f32)
        s["sq"][b, i] = jnp.broadcast_to(jnp.sum(mixed * mixed, axis=1, keepdims=True), (RX, 128))
        c = z_share(s["sq"].at[b])
        yield
        wait(c)
        square = s["sq"][b, 0]
        for k in range(1, 8):
            square = square + s["sq"][b, k]
        out_scale = lax.rsqrt(square[:, :1] / (8 * CW) + EPS)
        s["rsd"][b, q] = (s["xf"][own_x, :][:, :CW] + mixed * out_scale * post).astype(bf16)
        c = xy_gather(s["rsd"].at[b])
        yield
        wait(c)
        yield from mp_and_tp_sum(b, 0, merge(s["rsd"][b], R), ew_ref)
        pre_act = z_total(s["pe"][0, b, i], s["re"].at[0, b]) + s["eb"][:, half]
        active = jnp.maximum(pre_act, 0.0)
        s["act"][b] = active
        s["fe"][b, m, i] = (active * active).astype(bf16)
        yield from z_gather(s["fe"].at[b, m])
        c = send([(s["fe"].at[b, m], s["fe"].at[b, m], to_m)], s["fe"].at[b, 0])
        yield
        wait(c)
        recon = dot(merge(s["fe"][b, 0], R), dw_ref[:, :HL], LAST)
        recon = recon + dot(merge(s["fe"][b, 1], R), dw_ref[:, HL:], LAST)
        c = lat_sum(b, 1, recon)
        yield
        wait(c)
        s["hs"][1, b] = total(s["pm"][1, b, q], s["rm"].at[1, b], 16).astype(bf16)
        c = send([(s["hs"].at[1, b], s["hr"].at[1, b], to_h)], s["hr"].at[1, b])
        yield
        wait(c)
        error = s["hs"][1, b].astype(f32) + s["hr"][1, b].astype(f32) + dbias - s["rsd"][b, q].astype(f32)
        s["err"][b, q] = (2.0 * s["wrow"][own_x, :][:, :1] * error).astype(bf16)
        c = xy_gather(s["err"].at[b])
        yield
        wait(c)
        known.append(b)
        yield from mp_and_tp_sum(b, 1, merge(s["err"][b], R), dw_ref)
        norm_total = s["cn"][0, :, half] + s["cn"][1, :, half]
        grad = z_total(s["pe"][1, b, i], s["re"].at[1, b]) + s["wrow"][own_z, :][:, :1] * norm_total
        s["pd"][b, m, i] = (grad * 2.0 * s["act"][b]).astype(bf16)
        yield from z_gather(s["pd"].at[b, m])
        c = send([(s["pd"].at[b, m], s["pd"].at[b, m], to_m)], s["pd"].at[b, 0])
        yield
        wait(c)

    out_copies = []
    known = []
    running = [(b, block(b)) for b in range(NB)]
    phase = 0
    while running:
        running = [(b, g) for b, g in running if next(g, True) is None]
        phase += 1
        if phase == 2:
            wait(norm_copies)
            squares = s["nsq"][0]
            for k in range(1, 8):
                squares = squares + s["nsq"][k]
            s["cn"][m] = jnp.sqrt(squares + EPS)
            cn_copy = send([(s["cn"].at[m], s["cn"].at[m], to_m)], s["cn"].at[0])
        if phase == 3:
            cn_copy.wait_recv()
        if len(known) == NB:
            known.append(NB)
            err = merge(s["err"][...], ROWS)
            own_norm = s["cn"][m]
            for p in range(2):
                at = slice(p * HL, (p + 1) * HL)
                feats = s["fe"][:, p].astype(f32).reshape(ROWS, HL)
                weighted = jnp.sum(s["wrow"][:, :1] * feats, axis=0, keepdims=True)
                direct = dot(err, feats.astype(bf16), FIRST)
                dg_ref[:, at] = (
                    direct + weighted * dw_ref[:, at].astype(f32) / own_norm[:, at]).astype(bf16)
            out_copies.append(local_copy(dg_ref, dg_hbm.at[0], 5))

    resid = merge(s["rsd"][...], ROWS)
    for p in range(2):
        at = slice(p * HL, (p + 1) * HL)
        eg_ref[:, at] = dot(resid, merge(s["pd"][:, p], ROWS), FIRST).astype(bf16)
        out_copies.append(local_copy(eg_ref.at[:, at], eg_hbm.at[0, :, at], 6 + p))
    for c in sends:
        c.wait_send()

    @pl.when(at_edge)
    def _():
        link(edge_n, s["edge"], s["edge"], to_m).wait_send()

    for c in out_copies:
        c.wait()


def local(*args):
    vmem = pl.BlockSpec(memory_space=pltpu.VMEM)
    any_ = pl.BlockSpec(memory_space=pl.ANY)
    out = jax.ShapeDtypeStruct((1, CW, LW), bf16)
    return pl.pallas_call(
        kernel,
        out_shape=(out, out),
        in_specs=[any_ if n in (2, 3, 4, 6, 8) else vmem for n in range(13)],
        out_specs=(any_, any_),
        scratch_shapes=list(SCRATCH.values()),
        compiler_params=pltpu.CompilerParams(
            collective_id=1, has_side_effects=True, vmem_limit_bytes=56 << 20),
        cost_estimate=pl.CostEstimate(flops=2300000000, bytes_accessed=7000000, transcendentals=100000),
    )(*args)


def solution(mesh):
    placed = (
        P("mp", "lat", None),
        P("mp", None),
        P("mp", "lat", "tp"),
        P("mp", "lat", "tp"),
        P("mp", "lat", "tp"),
        P("mp", "tp"),
        P("mp", "tp", "lat"),
        P("lat"),
        P("mp", "tp", "lat"),
        P("mp", "tp"),
        P(),
        P(),
        P(),
    )
    return jax.shard_map(
        local,
        mesh=mesh,
        in_specs=placed,
        out_specs=(P("mp", "tp", "lat"), P("mp", "tp", "lat")),
        check_vma=False,
    )
```

```python
import functools

import jax
import jax.numpy as jnp
from jax import lax
from jax.experimental import pallas as pl
from jax.experimental.pallas import tpu as pltpu
from jax.sharding import PartitionSpec as P

MESH = pl.DeviceIdType.MESH
f32, bf16 = jnp.float32, jnp.bfloat16
EPS = 1e-06
NB = 3
ROWS = 384
R = ROWS // NB
RZ = R // 8
RX = R // 16
CW = 448
LW = 1024
HL = 512

LAST = (((1,), (1,)), ((), ()))
PLAIN = (((1,), (0,)), ((), ()))
FIRST = (((0,), (0,)), ((), ()))


def dot(a, b, dims=PLAIN):
    return lax.dot_general(a, b, dims, preferred_element_type=f32)


def merge(v, rows):
    return v.astype(f32).reshape(rows, v.shape[-1]).astype(bf16)


SCRATCH = {
    "edge": pltpu.VMEM((4, 12, 512), bf16),
    "nx": pltpu.VMEM((2, 16, 12, 512), bf16),
    "xf": pltpu.VMEM((ROWS, 512), f32),
    "wgu": pltpu.VMEM((2 * CW, CW), bf16),
    "wrow": pltpu.VMEM((ROWS, 128), f32),
    "nsq": pltpu.VMEM((8, 1, LW), f32),
    "cn": pltpu.VMEM((2, 1, LW), f32),
    "pg": pltpu.VMEM((NB, 8, RZ, 2 * CW), bf16),
    "rg": pltpu.VMEM((NB, 8, RZ, 2 * CW), bf16),
    "hd": pltpu.VMEM((NB, 8, RZ, CW), bf16),
    "pm": pltpu.VMEM((2, NB, 16, RX, CW), bf16),
    "rm": pltpu.VMEM((2, NB, 16, RX, CW), bf16),
    "hs": pltpu.VMEM((2, NB, RX, CW), bf16),
    "hr": pltpu.VMEM((2, NB, RX, CW), bf16),
    "sq": pltpu.VMEM((NB, 8, RX, 128), f32),
    "rsd": pltpu.VMEM((NB, 16, RX, CW), bf16),
    "err": pltpu.VMEM((NB, 16, RX, CW), bf16),
    "ms": pltpu.VMEM((2, NB, R, HL), bf16),
    "mr": pltpu.VMEM((2, NB, R, HL), bf16),
    "pe": pltpu.VMEM((2, NB, 8, RZ, HL), bf16),
    "re": pltpu.VMEM((2, NB, 8, RZ, HL), bf16),
    "act": pltpu.VMEM((NB, RZ, HL), f32),
    "fe": pltpu.VMEM((NB, 2, 8, RZ, HL), bf16),
    "pd": pltpu.VMEM((NB, 2, 8, RZ, HL), bf16),
    "wd": pltpu.VMEM((CW, CW), bf16),
    "ew": pltpu.VMEM((CW, LW), bf16),
    "dw": pltpu.VMEM((CW, LW), bf16),
    "eg": pltpu.VMEM((CW, LW), bf16),
    "dg": pltpu.VMEM((CW, LW), bf16),
    "eb": pltpu.VMEM((1, LW), f32),
    "load": pltpu.SemaphoreType.DMA((8,)),
    "sem": pltpu.SemaphoreType.DMA((2, 32 * NB + 6)),
}


def kernel(*refs):
    (x_ref, pre_ref, wg_hbm, wu_hbm, wd_hbm, post_ref, ew_hbm, eb_ref, dw_hbm, db_ref,
     prompt_ref, pad_ref, ids_ref, eg_hbm, dg_hbm) = refs[:15]
    s = dict(zip(SCRATCH, refs[15:]))
    wd_ref, ew_ref, dw_ref, eg_ref, dg_ref = s["wd"], s["ew"], s["dw"], s["eg"], s["dg"]
    sem = s["sem"]
    m, i, lat = lax.axis_index("mp"), lax.axis_index("tp"), lax.axis_index("lat")
    q, h = lax.div(lat, 2), lax.rem(lat, 2)
    to_z = [{"tp": lax.rem(i + k, 8)} for k in range(1, 8)]
    to_q = [lax.rem(q + k, 16) for k in range(1, 16)]
    to_xy = [{"lat": 2 * p + h} for p in to_q]
    to_h = {"lat": 2 * q + 1 - h}
    to_m = {"mp": 1 - m}

    gate = pltpu.get_barrier_semaphore()
    other_lat = 2 * q + 1 - h
    nearest = {"tp": jnp.where(i < 4, 7, 0), "lat": other_lat}
    at_edge = jnp.logical_or(i == 0, i == 7)
    everyone = to_z + to_xy + [to_h, to_m, nearest]
    for d in everyone:
        pl.semaphore_signal(gate, inc=1, device_id=d, device_id_type=MESH)

    def local_copy(src, dst, n):
        c = pltpu.make_async_copy(src, dst, s["load"].at[n])
        c.start()
        return c

    load_d = local_copy(dw_hbm.at[0], dw_ref, 0)
    load_g = [local_copy(wg_hbm.at[0], s["wgu"].at[pl.ds(0, CW)], 1),
              local_copy(wu_hbm.at[0], s["wgu"].at[pl.ds(CW, CW)], 2)]
    load_w = [local_copy(wd_hbm.at[0], wd_ref, 3), local_copy(ew_hbm.at[0], ew_ref, 4)]
    used, sends = [0], []

    def link(n, src, dst, where):
        return pltpu.make_async_remote_copy(
            src_ref=src, dst_ref=dst, send_sem=sem.at[0, n], recv_sem=sem.at[1, n],
            device_id=where, device_id_type=MESH)

    def send(copies, whole):
        n = used[0]
        used[0] += 1
        for src, dst, where in copies:
            link(n, src, dst, where).start()
        sends.append(link(n, whole, whole, to_m))
        return sends[-1]

    def wait(*groups):
        for c in groups:
            c.wait_recv()

    side, place = lax.div(i, 4), lax.rem(i, 4)
    mates = [lax.rem(place + k, 4) for k in range(1, 4)]
    to_mate = [{"tp": 4 * side + p} for p in mates]
    across = lax.rem(i + 4, 8)
    to_across = {"tp": across}

    def z_scatter(src, dst):
        far = send([(src.at[4 - 4 * side + p], dst.at[k], to_mate[k - 1])
                    for k, p in enumerate(mates, 1)], dst.at[pl.ds(1, 3)])
        yield
        wait(far)
        src[across] = (src[across].astype(f32) + dst[1].astype(f32)
                       + dst[2].astype(f32) + dst[3].astype(f32)).astype(bf16)
        last = send([(src.at[across], dst.at[4], to_across)], dst.at[4])
        near = send([(src.at[4 * side + p], dst.at[4 + k], to_mate[k - 1])
                     for k, p in enumerate(mates, 1)], dst.at[pl.ds(5, 3)])
        yield
        wait(near, last)

    def z_gather(ref):
        first = send([(ref.at[i], ref.at[i], to_across)], ref.at[0])
        near = send([(ref.at[i], ref.at[i], d) for d in to_mate], ref.at[pl.ds(0, 3)])
        yield
        wait(first)
        far = send([(ref.at[across], ref.at[across], d) for d in to_mate], ref.at[pl.ds(0, 3)])
        yield
        wait(near, far)

    def z_share(ref):
        return send([(ref.at[i], ref.at[i], d) for d in to_z], ref.at[pl.ds(0, 7)])

    def z_total(own, ref):
        acc = own.astype(f32)
        for k in range(4, 8):
            acc = acc + ref[k].astype(f32)
        return acc

    def xy_scatter(src, dst):
        return send([(src.at[to_q[k - 1]], dst.at[k], to_xy[k - 1]) for k in range(1, 16)],
                    dst.at[pl.ds(1, 15)])

    def xy_gather(ref):
        return send([(ref.at[q], ref.at[q], d) for d in to_xy], ref.at[pl.ds(0, 15)])

    def total(own, ref, count):
        acc = own.astype(f32)
        for k in range(1, count):
            acc = acc + ref[k].astype(f32)
        return acc

    x = x_ref[0].astype(f32)
    scale = lax.rsqrt(jnp.sum(x * x, axis=1, keepdims=True) / (8 * CW) + EPS)
    p0 = scale.astype(bf16).astype(f32)
    p1 = (scale - p0).astype(bf16).astype(f32)
    p2 = scale - p0 - p1
    lane = lax.broadcasted_iota(jnp.int32, (12, 512), 1)

    def payload(cols):
        wide = jnp.concatenate([cols, jnp.zeros((12, 64), f32)], axis=1)
        wide = jnp.where(lane == CW, p0, jnp.where(lane == CW + 1, p1, jnp.where(lane == CW + 2, p2, wide)))
        return wide.astype(bf16)

    cols = jnp.zeros((12, CW), f32)
    gain_in = jnp.zeros((1, CW), f32)
    pre = pre_ref[...].astype(f32)
    for c in range(8):
        cols = jnp.where(i == c, x[:, c * CW:(c + 1) * CW], cols)
        gain_in = jnp.where(i == c, pre[:, c * CW:(c + 1) * CW], gain_in)
    s["nx"][h, q] = payload(cols)
    for edge, low in ((7, 0), (0, 4)):
        @pl.when(i == edge)
        def _():
            for c in range(4):
                s["edge"][c] = payload(x[:, (low + c) * CW:(low + c + 1) * CW])

    pl.semaphore_wait(gate, jnp.where(at_edge, len(everyone) + 3, len(everyone) - 1))

    edge_n = used[0]
    used[0] += 1
    for edge, low in ((7, 0), (0, 4)):
        @pl.when(i == edge)
        def _():
            for c in range(4):
                link(edge_n, s["edge"].at[c], s["nx"].at[h, q], {"tp": low + c, "lat": other_lat}).start()

    def rows_gather(part):
        return send([(part.at[q], part.at[q], d) for d in to_xy], part.at[pl.ds(0, 15)])

    own_copies = rows_gather(s["nx"].at[h])
    load_d.wait()
    dw = dw_ref[...].astype(f32)
    s["nsq"][i] = jnp.sum(dw * dw, axis=0, keepdims=True)
    link(edge_n, s["nx"].at[0, 0], s["nx"].at[0, 0], to_m).wait_recv()
    other_copies = rows_gather(s["nx"].at[1 - h])
    norm_copies = z_share(s["nsq"])

    def column(v):
        return jnp.broadcast_to(v, (128, v.shape[1])).T[:, :1]

    prompt = column(prompt_ref[...].reshape(1, ROWS))
    valid = column(pad_ref[...].reshape(1, ROWS).astype(f32))
    in_prompt = prompt == lax.broadcasted_iota(jnp.int32, (ROWS, 96), 1)
    pair_of_prompt = lax.shift_right_logical(ids_ref[...].reshape(1, 96), 1).astype(f32)
    pair = jnp.sum(jnp.where(in_prompt, pair_of_prompt, 0.0), axis=1, keepdims=True)
    in_pair = pair == lax.broadcasted_iota(jnp.int32, (ROWS, 48), 1).astype(f32)
    counts = jnp.sum(jnp.where(in_pair, valid, 0.0), axis=0, keepdims=True)
    inverse = 1.0 / jnp.maximum(counts, 1.0)
    wrow = valid * jnp.sum(jnp.where(in_pair, inverse, 0.0), axis=1, keepdims=True)
    s["wrow"][...] = jnp.broadcast_to(wrow, (ROWS, 128))

    s["eb"][...] = eb_ref[...].astype(f32).reshape(1, LW)
    post = post_ref[...].astype(f32)
    dbias = db_ref[...].astype(f32)
    half = pl.ds(pl.multiple_of(m * HL, HL), HL)
    other = pl.ds(pl.multiple_of((1 - m) * HL, HL), HL)

    for c in load_g + load_w:
        c.wait()
    wait(own_copies, other_copies)
    for c in range(32):
        s["xf"][12 * c:12 * (c + 1)] = s["nx"][c % 2, c // 2].astype(f32)

    def mp_and_tp_sum(b, t, left, weight):
        s["ms"][t, b] = dot(left, weight[:, other]).astype(bf16)
        c = send([(s["ms"].at[t, b], s["mr"].at[t, b], to_m)], s["mr"].at[t, b])
        mine = dot(left, weight[:, half])
        yield
        c.wait_recv()
        both = mine + s["mr"][t, b].astype(f32)
        s["pe"][t, b] = both.reshape(8, RZ, HL).astype(bf16)
        yield from z_scatter(s["pe"].at[t, b], s["re"].at[t, b])

    def lat_sum(b, t, part):
        s["pm"][t, b] = part.reshape(16, RX, CW).astype(bf16)
        return xy_scatter(s["pm"].at[t, b], s["rm"].at[t, b])

    def block(b):
        rows = slice(b * R, (b + 1) * R)
        own_x = pl.ds(pl.multiple_of(b * R + q * RX, 8), RX)
        own_z = pl.ds(pl.multiple_of(b * R + i * RZ, 8), RZ)
        xb = s["xf"][rows]
        row_scale = xb[:, CW:CW + 1] + xb[:, CW + 1:CW + 2] + xb[:, CW + 2:CW + 3]
        normed = (xb[:, :CW] * row_scale * gain_in).astype(bf16)
        s["pg"][b] = dot(normed, s["wgu"][...], LAST).reshape(8, RZ, 2 * CW).astype(bf16)
        yield from z_scatter(s["pg"].at[b], s["rg"].at[b])
        both = z_total(s["pg"][b, i], s["rg"].at[b])
        g, u = both[:, :CW], both[:, CW:]
        s["hd"][b, i] = (0.5 * g * (1.0 + jnp.tanh(0.7978845608028654 * (g + 0.044715 * g * g * g))) * u).astype(bf16)
        yield from z_gather(s["hd"].at[b])
        c = lat_sum(b, 0, dot(merge(s["hd"][b], R), wd_ref[...]))
        yield
        wait(c)
        s["hs"][0, b] = total(s["pm"][0, b, q], s["rm"].at[0, b], 16).astype(bf16)
        c = send([(s["hs"].at[0, b], s["hr"].at[0, b], to_h)], s["hr"].at[0, b])
        yield
        wait(c)
        mixed = s["hs"][0, b].astype(f32) + s["hr"][0, b].astype(f32)
        s["sq"][b, i] = jnp.broadcast_to(jnp.sum(mixed * mixed, axis=1, keepdims=True), (RX, 128))
        c = z_share(s["sq"].at[b])
        yield
        wait(c)
        square = s["sq"][b, 0]
        for k in range(1, 8):
            square = square + s["sq"][b, k]
        out_scale = lax.rsqrt(square[:, :1] / (8 * CW) + EPS)
        s["rsd"][b, q] = (s["xf"][own_x, :][:, :CW] + mixed * out_scale * post).astype(bf16)
        c = xy_gather(s["rsd"].at[b])
        yield
        wait(c)
        yield from mp_and_tp_sum(b, 0, merge(s["rsd"][b], R), ew_ref)
        pre_act = z_total(s["pe"][0, b, i], s["re"].at[0, b]) + s["eb"][:, half]
        active = jnp.maximum(pre_act, 0.0)
        s["act"][b] = active
        s["fe"][b, m, i] = (active * active).astype(bf16)
        yield from z_gather(s["fe"].at[b, m])
        c = send([(s["fe"].at[b, m], s["fe"].at[b, m], to_m)], s["fe"].at[b, 0])
        yield
        wait(c)
        recon = dot(merge(s["fe"][b, 0], R), dw_ref[:, :HL], LAST)
        recon = recon + dot(merge(s["fe"][b, 1], R), dw_ref[:, HL:], LAST)
        c = lat_sum(b, 1, recon)
        yield
        wait(c)
        s["hs"][1, b] = total(s["pm"][1, b, q], s["rm"].at[1, b], 16).astype(bf16)
        c = send([(s["hs"].at[1, b], s["hr"].at[1, b], to_h)], s["hr"].at[1, b])
        yield
        wait(c)
        error = s["hs"][1, b].astype(f32) + s["hr"][1, b].astype(f32) + dbias - s["rsd"][b, q].astype(f32)
        s["err"][b, q] = (2.0 * s["wrow"][own_x, :][:, :1] * error).astype(bf16)
        c = xy_gather(s["err"].at[b])
        yield
        wait(c)
        known.append(b)
        yield from mp_and_tp_sum(b, 1, merge(s["err"][b], R), dw_ref)
        norm_total = s["cn"][0, :, half] + s["cn"][1, :, half]
        grad = z_total(s["pe"][1, b, i], s["re"].at[1, b]) + s["wrow"][own_z, :][:, :1] * norm_total
        s["pd"][b, m, i] = (grad * 2.0 * s["act"][b]).astype(bf16)
        yield from z_gather(s["pd"].at[b, m])
        c = send([(s["pd"].at[b, m], s["pd"].at[b, m], to_m)], s["pd"].at[b, 0])
        yield
        wait(c)

    out_copies = []
    known = []
    running = [(b, block(b)) for b in range(NB)]
    phase = 0
    while running:
        running = [(b, g) for b, g in running if next(g, True) is None]
        phase += 1
        if phase == 2:
            wait(norm_copies)
            squares = s["nsq"][0]
            for k in range(1, 8):
                squares = squares + s["nsq"][k]
            s["cn"][m] = jnp.sqrt(squares + EPS)
            cn_copy = send([(s["cn"].at[m], s["cn"].at[m], to_m)], s["cn"].at[0])
        if phase == 3:
            cn_copy.wait_recv()
        if len(known) == NB:
            known.append(NB)
            err = merge(s["err"][...], ROWS)
            own_norm = s["cn"][m]
            for p in range(2):
                at = slice(p * HL, (p + 1) * HL)
                feats = s["fe"][:, p].astype(f32).reshape(ROWS, HL)
                weighted = jnp.sum(s["wrow"][:, :1] * feats, axis=0, keepdims=True)
                direct = dot(err, feats.astype(bf16), FIRST)
                dg_ref[:, at] = (
                    direct + weighted * dw_ref[:, at].astype(f32) / own_norm[:, at]).astype(bf16)
            out_copies.append(local_copy(dg_ref, dg_hbm.at[0], 5))

    resid = merge(s["rsd"][...], ROWS)
    for p in range(2):
        at = slice(p * HL, (p + 1) * HL)
        eg_ref[:, at] = dot(resid, merge(s["pd"][:, p], ROWS), FIRST).astype(bf16)
        out_copies.append(local_copy(eg_ref.at[:, at], eg_hbm.at[0, :, at], 6 + p))
    for c in sends:
        c.wait_send()

    @pl.when(at_edge)
    def _():
        link(edge_n, s["edge"], s["edge"], to_m).wait_send()

    for c in out_copies:
        c.wait()


def local(*args):
    vmem = pl.BlockSpec(memory_space=pltpu.VMEM)
    any_ = pl.BlockSpec(memory_space=pl.ANY)
    out = jax.ShapeDtypeStruct((1, CW, LW), bf16)
    return pl.pallas_call(
        kernel,
        out_shape=(out, out),
        in_specs=[any_ if n in (2, 3, 4, 6, 8) else vmem for n in range(13)],
        out_specs=(any_, any_),
        scratch_shapes=list(SCRATCH.values()),
        compiler_params=pltpu.CompilerParams(
            collective_id=1, has_side_effects=True, vmem_limit_bytes=56 << 20),
        cost_estimate=pl.CostEstimate(flops=2300000000, bytes_accessed=7000000, transcendentals=100000),
    )(*args)


def solution(mesh):
    placed = (
        P("mp", "lat", None),
        P("mp", None),
        P("mp", "lat", "tp"),
        P("mp", "lat", "tp"),
        P("mp", "lat", "tp"),
        P("mp", "tp"),
        P("mp", "tp", "lat"),
        P("lat"),
        P("mp", "tp", "lat"),
        P("mp", "tp"),
        P(),
        P(),
        P(),
    )
    return jax.shard_map(
        local,
        mesh=mesh,
        in_specs=placed,
        out_specs=(P("mp", "tp", "lat"), P("mp", "tp", "lat")),
        check_vma=False,
    )
```
